128 devices in a mesh: gx: 4 (over z_lo, core), gy: 4 (over y), gz: 8 (over x, z_hi).
Axes of the slice: x: 4, y: 4, z: 4 (z_hi: 2, z_lo: 2; z = z_hi * 2 + z_lo), core: 2. Of those that a mesh axis runs over, the one named last changes fastest.
Arguments:
- right_side: float32 [4, 4, 4, 16, 16, 1024], P(None, None, None, 'gx', 'gy', 'gz'), may hold values from -6 to 6
- mass_coef: float32 [16, 16, 1024], P('gx', 'gy', 'gz'), may hold values from 0.5 to 5
- conductivity: float32 [16, 16, 1024], P('gx', 'gy', 'gz'), may hold values from 0.3 to 3
- block_inverse: bfloat16 [64, 64, 16, 16, 1024], P(None, None, 'gx', 'gy', 'gz'), may hold values from -0.12 to 1.25
- mass_ref: float32 [64, 64], replicated, may hold values from -0.2 to 1
- stiff_ref: float32 [64, 64], replicated, may hold values from -0.2 to 1
- face_mass: float32 [16, 16], replicated, may hold values from -0.1 to 0.3
- coarse_modes: float32 [64, 8], replicated, may hold values from -0.75 to 0.75
- elem_agg: int32 [16, 16, 1024], P('gx', 'gy', 'gz'), may hold values from 0 to 255, as said below
- coarse_diag: float32 [8, 8, 32768], P(None, None, ('gx', 'gy', 'gz')), may hold values from -4 to 8
- coarse_inv: float32 [8, 8, 32768], P(None, None, ('gx', 'gy', 'gz')), may hold values from -0.2 to 0.5
- coarse_weight: float32 [6, 32768], P(None, ('gx', 'gy', 'gz')), may hold values from 0.1 to 0.6
- coarse_links: int32 [6, 32768], P(None, ('gx', 'gy', 'gz')), may hold values from 0 to 32768, as said below
Outputs:
- solution: float32 [4, 4, 4, 16, 16, 1024], P(None, None, None, 'gx', 'gy', 'gz')
- final_residual: float32 [4, 4, 4, 16, 16, 1024], P(None, None, None, 'gx', 'gy', 'gz')
The draws below stay inside these ranges and needn't reach their ends.
Inputs may be any that keep to these rules, and one draw needn't show every extreme that they name: `elem_agg`: the aggregate lies in the element's own device block of 4 x 4 x 128 elements; every aggregate number of a block is used. `coarse_links`: global aggregate numbers as in agg_id; 32768 where a face has no neighbour.
All inputs are finite; a program needn't handle non-finite values.
Results may differ from the reference program's by a relative error of at most 0.024.
Values sent between devices are 32-bit elements; how exact they have to be, the bound alone decides.
A program may use at most 320 MiB of HBM per device.

```python
import math
import jax
import jax.numpy as jnp
from jax import lax

EX = 4
EY = 4
EZ = 128
NC = 8
CYCLES = 2
SWEEPS = 2
AGG_DEV = 256
NX = 16
NY = 16
NZ = 1024
NAGG = 32768


def coefficients(key):
    shape_all = (NX, NY, NZ)
    mass_val = jnp.exp(jax.random.uniform(jax.random.fold_in(key, 101), shape_all, jnp.float32, jnp.log(0.5), jnp.log(5.0)))
    kappa_val = jnp.exp(jax.random.uniform(jax.random.fold_in(key, 102), shape_all, jnp.float32, jnp.log(0.3), jnp.log(3.0)))
    return (mass_val, kappa_val)


def coarse_scale(key):
    return jnp.exp(jax.random.uniform(jax.random.fold_in(key, 103), (NAGG,), jnp.float32, jnp.log(2.0), jnp.log(8.0)))


def near_identity(key, order, spread):
    identity = jnp.eye(order, dtype=jnp.float32)
    jitter = jnp.clip(jax.random.normal(key, (order, order), jnp.float32), -4.0, 4.0) * spread
    return identity + (1.0 - identity) * jitter


def draw_mass_coef(key, part):
    mass_val, kappa_val = coefficients(key)
    return mass_val


def draw_conductivity(key, part):
    mass_val, kappa_val = coefficients(key)
    return kappa_val


def draw_block_inverse(key, part):
    mass_val, kappa_val = coefficients(key)
    key = jax.random.fold_in(key, 3)
    identity = jnp.eye(64, dtype=jnp.float32)[:, :, None, None, None]
    jitter = jnp.clip(jax.random.normal(key, (64, 64, NX, NY, NZ), jnp.float32), -3.0, 3.0) * 0.03
    return ((identity + (1.0 - identity) * jitter) / (mass_val + kappa_val)[None, None]).astype(jnp.bfloat16)


def draw_mass_ref(key, part):
    key = jax.random.fold_in(key, 4)
    return near_identity(key, 64, 0.04)


def draw_stiff_ref(key, part):
    key = jax.random.fold_in(key, 5)
    return near_identity(key, 64, 0.045)


def draw_face_mass(key, part):
    key = jax.random.fold_in(key, 6)
    return 0.3 * near_identity(key, 16, 0.06)


def draw_coarse_diag(key, part):
    scales = coarse_scale(key)
    key = jax.random.fold_in(key, 7)
    identity = jnp.eye(NC, dtype=jnp.float32)[:, :, None]
    jitter = jnp.clip(jax.random.normal(key, (NC, NC, NAGG), jnp.float32), -4.0, 4.0) * 0.1
    return (identity + (1.0 - identity) * jitter) * scales[None, None]


def draw_coarse_inv(key, part):
    scales = coarse_scale(key)
    key = jax.random.fold_in(key, 9)
    identity = jnp.eye(NC, dtype=jnp.float32)[:, :, None]
    jitter = jnp.clip(jax.random.normal(key, (NC, NC, NAGG), jnp.float32), -4.0, 4.0) * 0.1
    return (identity + (1.0 - identity) * jitter) / scales[None, None]


def draw_elem_agg(key, part):
    key = jax.random.fold_in(key, 8)
    shape_all = (NX, NY, NZ)
    coord_x = lax.broadcasted_iota(jnp.int32, shape_all, 0) % EX
    coord_y = lax.broadcasted_iota(jnp.int32, shape_all, 1) % EY
    coord_z = lax.broadcasted_iota(jnp.int32, shape_all, 2) % EZ
    base_id = (coord_x // 2 * (EY // 2) + coord_y // 2) * (EZ // 2) + coord_z // 2
    corner = (coord_x % 2 == 0) & (coord_y % 2 == 0) & (coord_z % 2 == 0)
    chosen = jax.random.randint(jax.random.fold_in(key, 1), shape_all, 0, 4)
    random_id = jax.random.randint(jax.random.fold_in(key, 2), shape_all, 0, AGG_DEV)
    return jnp.where((chosen == 0) & jnp.logical_not(corner), random_id, base_id).astype(jnp.int32)


def draw_coarse_links(key, part):
    key = jax.random.fold_in(key, 10)
    numbers = jnp.arange(NAGG, dtype=jnp.int32)
    device = numbers // AGG_DEV
    within = numbers % AGG_DEV
    half_x = EX // 2
    half_y = EY // 2
    half_z = EZ // 2
    grid_y = NY // EY
    grid_z = NZ // EZ
    dev_x = device // (grid_y * grid_z)
    dev_y = device // grid_z % grid_y
    dev_z = device % grid_z
    loc_x = within // (half_y * half_z)
    loc_y = within // half_z % half_y
    loc_z = within % half_z
    coords = [dev_x * half_x + loc_x, dev_y * half_y + loc_y, dev_z * half_z + loc_z]
    bounds = [NX // 2, NY // 2, NZ // 2]
    listed = []
    for axis_id in range(3):
        for offset_step in (-1, 1):
            shifted = list(coords)
            shifted[axis_id] = shifted[axis_id] + offset_step
            inside = (shifted[axis_id] >= 0) & (shifted[axis_id] < bounds[axis_id])
            near_dev = (shifted[0] // half_x * grid_y + shifted[1] // half_y) * grid_z + shifted[2] // half_z
            near_local = (shifted[0] % half_x * half_y + shifted[1] % half_y) * half_z + shifted[2] % half_z
            listed.append(jnp.where(inside, near_dev * AGG_DEV + near_local, NAGG))
    link_ids = jnp.stack(listed).astype(jnp.int32)
    chosen = jax.random.randint(jax.random.fold_in(key, 1), (6, NAGG), 0, 4)
    random_id = jax.random.randint(jax.random.fold_in(key, 2), (6, NAGG), 0, NAGG)
    return jnp.where((chosen == 0) & (link_ids < NAGG), random_id, link_ids).astype(jnp.int32)


def shard_levels(own_key, shape, shards, least, high):
    gain = 1.0
    for dim, parts in shards:
        draws = jax.random.uniform(jax.random.fold_in(jax.random.fold_in(own_key, 6), dim), (parts,), jnp.float32, least / len(shards), high / len(shards))
        gain = gain * jnp.repeat(jnp.exp(draws), shape[dim] // parts).reshape((-1,) + (1,) * (len(shape) - 1 - dim))
    return gain


def normal_values(key, extent, scale, most, split=(), kind=jnp.bfloat16):
    array = scale * jax.random.normal(key, extent, jnp.float32)
    if split:
        array = array * shard_levels(key, extent, split, -0.22, 0.18)
    return jnp.clip(array, -most, most).astype(kind)


def setup_inputs(seed: int = 0) -> dict:
    key_list = jax.random.split(jax.random.key(seed), 14)
    right_side = normal_values(key_list[0], (4, 4, 4, NX, NY, NZ), 1.0, 6.0, ((3, 4), (4, 4), (5, 8)), jnp.float32)
    mass_coef = draw_mass_coef(jax.random.fold_in(key_list[13], 71), 0)
    conductivity = draw_conductivity(jax.random.fold_in(key_list[13], 71), 0)
    block_inverse = draw_block_inverse(jax.random.fold_in(key_list[13], 71), 0)
    mass_ref = draw_mass_ref(jax.random.fold_in(key_list[13], 71), 0)
    stiff_ref = draw_stiff_ref(jax.random.fold_in(key_list[13], 71), 0)
    face_mass = draw_face_mass(jax.random.fold_in(key_list[13], 71), 0)
    coarse_modes = normal_values(key_list[7], (64, NC), 64 ** -0.5, 0.75, (), jnp.float32)
    elem_agg = draw_elem_agg(jax.random.fold_in(key_list[13], 71), 0)
    coarse_diag = draw_coarse_diag(jax.random.fold_in(key_list[13], 71), 0)
    coarse_inv = draw_coarse_inv(jax.random.fold_in(key_list[13], 71), 0)
    coarse_weight = jnp.clip(jnp.exp(math.log(0.6) - 1.7917595 * jax.random.uniform(key_list[11], (6, NAGG), jnp.float32) ** shard_levels(key_list[11], (6, NAGG), ((1, 128),), -0.2, 0.2)), 0.1, 0.6)
    coarse_links = draw_coarse_links(jax.random.fold_in(key_list[13], 71), 0)
    return dict(right_side=right_side, mass_coef=mass_coef, conductivity=conductivity, block_inverse=block_inverse, mass_ref=mass_ref, stiff_ref=stiff_ref, face_mass=face_mass, coarse_modes=coarse_modes, elem_agg=elem_agg, coarse_diag=coarse_diag, coarse_inv=coarse_inv, coarse_weight=coarse_weight, coarse_links=coarse_links)


damping = 0.8


def face_conductance(conductivity, padded):
    result = []
    for direction in range(3):
        interior = [slice(1, -1)] * 3
        lower_cut = list(interior)
        lower_cut[direction] = slice(0, -2)
        upper_cut = list(interior)
        upper_cut[direction] = slice(2, None)
        for beside in (padded[tuple(lower_cut)], padded[tuple(upper_cut)]):
            result.append(2.0 * conductivity * beside / (conductivity + beside))
    return result


def padded_neighbours(padded):
    listed = []
    for direction in range(3):
        upper_trace = jnp.take(padded, 3, axis=direction)
        lower_trace = jnp.take(padded, 0, axis=direction)
        interior = [slice(None), slice(None), slice(1, -1), slice(1, -1), slice(1, -1)]
        lower_cut = list(interior)
        lower_cut[2 + direction] = slice(0, -2)
        upper_cut = list(interior)
        upper_cut[2 + direction] = slice(2, None)
        listed.append(upper_trace[tuple(lower_cut)])
        listed.append(lower_trace[tuple(upper_cut)])
    return listed


def surface_terms(field_now, neighbours, conduct, face_mass):
    summed = jnp.zeros_like(field_now)
    for direction in range(3):
        for side_id in range(2):
            values_in = neighbours[2 * direction + side_id]
            shaped = values_in.reshape(16, -1)
            mapped = jnp.dot(face_mass, shaped, precision=lax.Precision.HIGHEST).reshape(values_in.shape)
            weighted = conduct[2 * direction + side_id] * mapped
            target = [slice(None)] * 6
            target[direction] = 3 * side_id
            summed = summed.at[tuple(target)].add(weighted)
    return summed


def local_operator(field_now, neighbours, conduct, mass_coef, conductivity, mass_ref, stiff_ref, face_mass):
    flattened = field_now.reshape(64, -1)
    massed = jnp.dot(mass_ref, flattened, precision=lax.Precision.HIGHEST).reshape(field_now.shape)
    stiffed = jnp.dot(stiff_ref, flattened, precision=lax.Precision.HIGHEST).reshape(field_now.shape)
    return mass_coef * massed + conductivity * stiffed - surface_terms(field_now, neighbours, conduct, face_mass)


def block_product(block_inverse, rounded):
    stacked = rounded.reshape(64, *rounded.shape[3:]).astype(jnp.float32)

    def one_slab(slab_id):
        blocks = lax.dynamic_index_in_dim(block_inverse, slab_id, 2, keepdims=False).astype(jnp.float32)
        column = lax.dynamic_index_in_dim(stacked, slab_id, 1, keepdims=False)
        return jnp.einsum("ijyz,jyz->iyz", blocks, column, precision=lax.Precision.HIGHEST)

    slab_list = lax.map(one_slab, jnp.arange(block_inverse.shape[2], dtype=jnp.int32))
    return jnp.moveaxis(slab_list, 0, 1).reshape(rounded.shape)


def coarse_apply(coarse_state, coarse_diag, coarse_weight, coarse_links):
    padded = jnp.concatenate([coarse_state, jnp.zeros((coarse_state.shape[0], 1), jnp.float32)], axis=1)
    nearby = padded[:, coarse_links]
    coupled = jnp.sum(coarse_weight[None] * nearby, axis=1)
    return jnp.einsum("ija,ja->ia", coarse_diag, coarse_state, precision=lax.Precision.HIGHEST) - coupled


def reference(right_side, mass_coef, conductivity, block_inverse, mass_ref, stiff_ref, face_mass, coarse_modes, elem_agg, coarse_diag, coarse_inv, coarse_weight, coarse_links):
    conduct = face_conductance(conductivity, jnp.pad(conductivity, 1))

    def operate(field_now):
        neighbours = padded_neighbours(jnp.pad(field_now, ((0, 0), (0, 0), (0, 0), (1, 1), (1, 1), (1, 1))))
        return local_operator(field_now, neighbours, conduct, mass_coef, conductivity, mass_ref, stiff_ref, face_mass)

    def smooth(field_now):
        defect = right_side - operate(field_now)
        rounded = defect.astype(jnp.bfloat16)
        return field_now + damping * block_product(block_inverse, rounded)

    coord_x = lax.broadcasted_iota(jnp.int32, (NX, NY, NZ), 0)
    coord_y = lax.broadcasted_iota(jnp.int32, (NX, NY, NZ), 1)
    coord_z = lax.broadcasted_iota(jnp.int32, (NX, NY, NZ), 2)
    device = ((coord_x // EX) * (NY // EY) + coord_y // EY) * (NZ // EZ) + coord_z // EZ
    agg_ids = (device * AGG_DEV + elem_agg).reshape(-1).astype(jnp.int32)

    solution = jnp.zeros_like(right_side)
    for cycle_id in range(CYCLES):
        for sweep_id in range(SWEEPS):
            solution = smooth(solution)
        residual = right_side - operate(solution)
        projected = jnp.dot(coarse_modes.T, residual.reshape(64, -1), precision=lax.Precision.HIGHEST)
        restricted = jax.ops.segment_sum(projected.T, agg_ids, NAGG).T
        coarse_state = jnp.zeros((NC, NAGG), jnp.float32)
        for sweep_id in range(SWEEPS):
            applied = coarse_apply(coarse_state, coarse_diag, coarse_weight, coarse_links)
            coarse_state = coarse_state + damping * jnp.einsum("ija,ja->ia", coarse_inv, restricted - applied, precision=lax.Precision.HIGHEST)
        correction = jnp.dot(coarse_modes, coarse_state[:, agg_ids], precision=lax.Precision.HIGHEST)
        solution = solution + correction.reshape(solution.shape)
        for sweep_id in range(SWEEPS):
            solution = smooth(solution)
    final_residual = right_side - operate(solution)
    return solution, final_residual
```

```python
import functools

import jax
import jax.numpy as jnp
from jax import lax
from jax.experimental import pallas as pl
from jax.experimental.pallas import tpu as pltpu
from jax.sharding import PartitionSpec as P

MESH = pl.DeviceIdType.MESH
F32 = jnp.float32
BF16 = jnp.bfloat16
damping = 0.8

XL, XU, YL, YU, ZL, ZU = range(6)
ROW_MASS, ROW_STIFF, ROW_XL, ROW_XU, ROW_YL, ROW_YU, ROW_ZL, ROW_ZU = 0, 64, 128, 144, 160, 192, 224, 240


def exact_dot(a, b, dims=(((1,), (0,)), ((), ()))):
    return lax.dot_general(a, b, dims, precision=lax.Precision.HIGHEST, preferred_element_type=F32)


def bf16_dot(a, b):
    return lax.dot_general(a, b, (((1,), (0,)), ((), ())), preferred_element_type=F32)


def split(value):
    high = value.astype(BF16)
    return high, (value - high.astype(F32)).astype(BF16)


def iota(shape, dim):
    return lax.broadcasted_iota(jnp.int32, shape, dim)


def stacked_operator(mass_ref, stiff_ref, face_mass):
    col = iota((64, 256), 1)
    row = iota((64, 256), 0)
    total = exact_dot(mass_ref, (col == row + ROW_MASS).astype(F32))
    total = total + exact_dot(stiff_ref, (col == row + ROW_STIFF).astype(F32))
    r, q = iota((64, 16), 0), iota((64, 16), 1)
    c, k = iota((16, 256), 0), iota((16, 256), 1)
    q_hi, q_lo = q // 4, q % 4
    c_hi, c_lo = c // 4, c % 4
    faces = (
        (q, ROW_XL + c),
        (48 + q, ROW_XU + c),
        (q_hi * 16 + q_lo, ROW_YL + c_hi * 8 + 4 + c_lo),
        (q_hi * 16 + 12 + q_lo, ROW_YU + c_hi * 8 + c_lo),
        (4 * q, ROW_ZL + c),
        (4 * q + 3, ROW_ZU + c),
    )
    for target, source in faces:
        placed = exact_dot((r == target).astype(F32), face_mass)
        total = total - exact_dot(placed, (k == source).astype(F32))
    return total


def kernel(
    rhs_in, mass_coef_in, kappa_in, block_inverse, mass_ref_in, stiff_ref_in, face_mass_in, modes_t_in, elem_agg_in,
    coarse_diag_in, coarse_inv_in, coarse_weight_in, coarse_links_in,
    sol_out, res_out,
    rhs, mass_coef, kappa, mass_ref, stiff_ref, face_mass, modes_t, elem_agg,
    coarse_diag, coarse_inv, coarse_weight, coarse_links,
    bvm, wm, dm, rhsm, rb, diag_t, inv_t, zhi, zlo, whl, coef, mem, mem_t, pj, rx, rz, sx, sz, krecv, held,
    in_sem, b_sem, k_send, k_recv, h_send, h_recv, g_send, g_recv, d_send, d_recv,
):
    gx, gy, gz = lax.axis_index("gx"), lax.axis_index("gy"), lax.axis_index("gz")
    core = gx % 2
    place = (gz // 2, gy, (gz % 2) * 2 + gx // 2)

    def device(chip, which):
        return ((chip[2] % 2) * 2 + which, chip[1], chip[0] * 2 + chip[2] // 2)

    def moved(dim, offset):
        return tuple((v + offset) % 4 if d == dim else v for d, v in enumerate(place))

    beside = (
        ((gx + 3) % 4, gy, gz), ((gx + 1) % 4, gy, gz),
        (gx, (gy + 3) % 4, gz), (gx, (gy + 1) % 4, gz),
        (gx, gy, (gz + 7) % 8), (gx, gy, (gz + 1) % 8),
    )
    sibling = device(place, 1 - core)
    peers = [[device(moved(dim, o), core) for o in (1, 2, 3)] for dim in range(3)]

    order = (0, 1, 2, 3, 12, 13, 14, 15, 4, 7, 8, 11, 5, 6, 9, 10)

    def block_copy(n):
        rows = pl.ds(4 * order[n], 4)
        return pltpu.make_async_copy(block_inverse.at[rows], bvm.at[rows], b_sem.at[n])

    arriving = [
        pltpu.make_async_copy(src, dst, in_sem.at[n])
        for n, (src, dst) in enumerate(
            (
                (kappa_in, kappa), (rhs_in, rhs), (mass_ref_in, mass_ref), (stiff_ref_in, stiff_ref),
                (face_mass_in, face_mass), (modes_t_in, modes_t), (elem_agg_in, elem_agg), (mass_coef_in, mass_coef),
                (coarse_diag_in, coarse_diag), (coarse_inv_in, coarse_inv),
                (coarse_weight_in, coarse_weight), (coarse_links_in, coarse_links),
            )
        )
    ]
    for copy in arriving:
        copy.start()
    for n in range(16):
        block_copy(n).start()

    barrier = pltpu.get_barrier_semaphore()
    greeted = list(beside) + [sibling] + [d for line in peers for d in line]
    for target in greeted:
        pl.semaphore_signal(barrier, inc=1, device_id=target, device_id_type=MESH)
    pl.semaphore_wait(barrier, len(greeted))

    def remote(src, dst, send, recv, target):
        return pltpu.make_async_remote_copy(
            src_ref=src, dst_ref=dst, send_sem=send, recv_sem=recv, device_id=target, device_id_type=MESH
        )

    def kappa_copy(f):
        return remote(kappa, krecv.at[f ^ 1], k_send.at[f], k_recv.at[f ^ 1], beside[f])

    arriving[0].wait()
    for f in range(6):
        kappa_copy(f).start()
    for copy in arriving[1:]:
        copy.wait()

    for xy in range(16):
        rhsm[pl.ds(xy * 64, 64), :] = rhs[pl.ds(xy, 64, stride=16), :]
    wm[...] = jnp.zeros_like(wm)
    high, low = split(stacked_operator(mass_ref[...], stiff_ref[...], face_mass[...]))
    whl[pl.ds(0, 64), :] = high
    whl[pl.ds(64, 64), :] = low
    turned = (iota((64, 64), 1) == iota((64, 64), 0) % 8 * 8 + iota((64, 64), 0) // 8).astype(F32)
    inv_t[...] = exact_dot(turned, coarse_inv[...])
    diag_t[...] = exact_dot(turned, coarse_diag[...])
    mt_hi, mt_lo = split(modes_t[...])
    eye64 = (iota((64, 64), 0) == iota((64, 64), 1)).astype(F32)
    modes = exact_dot(eye64, modes_t[...], (((1,), (1,)), ((), ())))
    agg = elem_agg[...]
    eye128 = (iota((128, 128), 0) == iota((128, 128), 1)).astype(F32)
    agg_t = exact_dot(eye128, agg.astype(F32), (((1,), (1,)), ((), ())))
    numbers = iota((128, 256), 1).astype(F32)
    numbers_t = iota((256, 128), 0)
    for xy in range(16):
        mem[pl.ds(xy * 128, 128), :] = (agg_t[:, xy : xy + 1] == numbers).astype(F32).astype(BF16)
        mem_t[:, pl.ds(xy * 128, 128)] = (agg[xy : xy + 1, :] == numbers_t).astype(F32).astype(BF16)

    for f in range(6):
        kappa_copy(f).wait()
    own = kappa[...]
    row, lane = iota((16, 128), 0), iota((16, 128), 1)
    down_x = jnp.concatenate([krecv[XL][12:16], own[0:12]], axis=0)
    up_x = jnp.concatenate([own[4:16], krecv[XU][0:4]], axis=0)
    down_y = jnp.where(row % 4 == 0, jnp.roll(krecv[YL], -3, 0), jnp.roll(own, 1, 0))
    up_y = jnp.where(row % 4 == 3, jnp.roll(krecv[YU], 3, 0), jnp.roll(own, -1, 0))
    down_z = jnp.where(lane == 0, pltpu.roll(krecv[ZL], 1, 1), pltpu.roll(own, 1, 1))
    up_z = jnp.where(lane == 127, pltpu.roll(krecv[ZU], 127, 1), pltpu.roll(own, 127, 1))
    outside = (
        (row < 4) & (gx == 0), (row >= 12) & (gx == 3),
        (row % 4 == 0) & (gy == 0), (row % 4 == 3) & (gy == 3),
        (lane == 0) & (gz == 0), (lane == 127) & (gz == 7),
    )
    coef[0] = mass_coef[...]
    coef[1] = own
    for f, near in enumerate((down_x, up_x, down_y, up_y, down_z, up_z)):
        near = jnp.where(outside[f], 0.0, near)
        coef[2 + f] = 2.0 * own * near / (own + near)

    half = iota((8, 128), 0) < 4
    lane16 = iota((16, 128), 1)

    def face_copy(f, slot):
        if f < 4:
            src, dst = sx.at[f], rx.at[slot, f ^ 1]
        else:
            src, dst = sz.at[f - 4], rz.at[slot, (f ^ 1) - 4]
        return remote(src, dst, h_send.at[f], h_recv.at[slot, f ^ 1], beside[f])

    def send_x(slot):
        for y in range(4):
            sx[XL, pl.ds(y * 16, 16), :] = wm[pl.ds(y * 64, 16), :]
            sx[XU, pl.ds(y * 16, 16), :] = wm[pl.ds((12 + y) * 64 + 48, 16), :]
        face_copy(XL, slot).start()
        face_copy(XU, slot).start()

    def send_y(slot):
        for x in range(4):
            for pair in range(2):
                at = 4 * x * 64 + pair * 32
                first, second = wm[pl.ds(at, 8), :], wm[pl.ds(at + 16, 8), :]
                sx[YL, pl.ds(x * 16 + pair * 8, 8), :] = jnp.where(half, first, pltpu.roll(second, 4, 0))
                at = (4 * x + 3) * 64 + pair * 32 + 8
                first, second = wm[pl.ds(at, 8), :], wm[pl.ds(at + 16, 8), :]
                sx[YU, pl.ds(x * 16 + pair * 8, 8), :] = jnp.where(half, pltpu.roll(first, 4, 0), second)
        face_copy(YL, slot).start()
        face_copy(YU, slot).start()

    def send_z(slot):
        lower = upper = jnp.zeros((16, 128), F32)
        for xy in range(16):
            first = wm[pl.ds(xy * 64, 16, stride=4), :]
            last = wm[pl.ds(xy * 64 + 3, 16, stride=4), :]
            lower = jnp.where(lane16 == xy, first[:, 0:1], lower)
            upper = jnp.where(lane16 == xy, last[:, 127:128], upper)
        sz[0] = lower
        sz[1] = upper
        face_copy(ZL, slot).start()
        face_copy(ZU, slot).start()

    def operate(slot):
        for f in range(6):
            face_copy(f, slot).wait()
        z_low, z_high = rz[slot, 0], rz[slot, 1]
        for xy in range(16):
            x, y = xy // 4, xy % 4
            pair, lanes = xy // 2, pl.ds(xy % 2 * 128, 128)

            def put(at, count, which, value):
                value = coef[which, pl.ds(xy, 1), :] * value
                high = value.astype(BF16)
                zhi[pair, pl.ds(at, count), lanes] = high
                zlo[pair, pl.ds(at, count), lanes] = (value - high.astype(F32)).astype(BF16)

            here = wm[pl.ds(xy * 64, 64), :]
            put(ROW_MASS, 64, 0, here)
            put(ROW_STIFF, 64, 1, here)
            put(ROW_XL, 16, 2, wm[pl.ds((xy - 4) * 64 + 48, 16), :] if x > 0 else rx[slot, XL, pl.ds(y * 16, 16), :])
            put(ROW_XU, 16, 3, wm[pl.ds((xy + 4) * 64, 16), :] if x < 3 else rx[slot, XU, pl.ds(y * 16, 16), :])
            if y > 0:
                low = [wm[pl.ds((xy - 1) * 64 + 16 * i + 8, 8), :] for i in range(4)]
            else:
                a, b = rx[slot, YL, pl.ds(x * 16, 8), :], rx[slot, YL, pl.ds(x * 16 + 8, 8), :]
                low = [pltpu.roll(a, 4, 0), a, pltpu.roll(b, 4, 0), b]
            put(ROW_YL, 32, 4, jnp.concatenate(low, axis=0))
            if y < 3:
                up = [wm[pl.ds((xy + 1) * 64 + 16 * i, 8), :] for i in range(4)]
            else:
                a, b = rx[slot, YU, pl.ds(x * 16, 8), :], rx[slot, YU, pl.ds(x * 16 + 8, 8), :]
                up = [a, pltpu.roll(a, 4, 0), b, pltpu.roll(b, 4, 0)]
            put(ROW_YU, 32, 5, jnp.concatenate(up, axis=0))
            below = pltpu.roll(wm[pl.ds(xy * 64 + 3, 16, stride=4), :], 1, 1)
            above = pltpu.roll(wm[pl.ds(xy * 64, 16, stride=4), :], 127, 1)
            put(ROW_ZL, 16, 6, jnp.where(lane16 == 0, z_low[:, xy : xy + 1], below))
            put(ROW_ZU, 16, 7, jnp.where(lane16 == 127, z_high[:, xy : xy + 1], above))
        for pair in range(8):
            both = bf16_dot(whl[...], zhi[pair])
            applied = both[0:64] + (both[64:128] + bf16_dot(whl[pl.ds(0, 64), :], zlo[pair]))
            for h in range(2):
                rows = pl.ds((2 * pair + h) * 64, 64)
                dm[rows, :] = rhsm[rows, :] - applied[:, h * 128 : h * 128 + 128]

    def block_rows(q):
        sums = [jnp.zeros((16, 128), F32) for _ in range(4)]
        for g in range(16):
            column = [rb[4 * g + j] for j in range(4)]
            for i in range(4):
                m = [bvm[4 * q + i, 4 * g + j] * column[j] for j in range(4)]
                sums[i] = sums[i] + ((m[0] + m[1]) + (m[2] + m[3])).astype(F32)
        for i in range(4):
            rows = pl.ds(4 * q + i, 16, stride=64)
            wm[rows, :] = wm[rows, :] + damping * sums[i]

    def sweep(slot, first):
        if first:
            for n in range(16):
                block_copy(n).wait()
                block_rows(order[n])
                if n == 7:
                    send_x(slot)
                if n == 11:
                    send_y(slot)
        else:
            pl.loop(0, 8)(lambda n: block_rows(n + 8 * (n // 4)))
            send_x(slot)
            pl.loop(0, 4)(lambda n: block_rows(4 + 4 * (n // 2) + 3 * (n % 2)))
            send_y(slot)
            pl.loop(0, 4)(lambda n: block_rows(5 + 4 * (n // 2) + n % 2))
        send_z(slot)

    routes = ((0, 1, 2), (1, 2, 0))

    def whole(cycle, half_id, which, done, chip):
        index = [slice(None) if d in done else chip[d] for d in range(3)]
        return held.at[cycle, which, index[2], index[1], index[0], half_id]

    def gather_copy(cycle, half_id, stage, o):
        route = routes[half_id]
        block = whole(cycle, half_id, core, route[:stage], place)
        at = (cycle, half_id, stage, o - 1)
        return remote(block, block, g_send.at[at], g_recv.at[at], peers[route[stage]][o - 1])

    def sibling_copy(cycle, half_id, o):
        route = routes[half_id]
        chip = moved(route[2], -o)
        block = whole(cycle, half_id, core, route[:2], chip)
        at = (cycle, half_id, o)
        return remote(block, block, d_send.at[at], d_recv.at[at], sibling)

    def collect(cycle, state):
        for h in range(2):
            held[cycle, core, place[2], place[1], place[0], h] = state[:, h * 128 : h * 128 + 128]
        for stage in range(3):
            for h in range(2):
                if stage > 0:
                    for o in (1, 2, 3):
                        gather_copy(cycle, h, stage - 1, o).wait_recv()
                for o in (1, 2, 3):
                    gather_copy(cycle, h, stage, o).start()
        for h in range(2):
            sibling_copy(cycle, h, 0).start()
        for o in (1, 3, 2):
            for h in range(2):
                gather_copy(cycle, h, 2, o).wait_recv()
                sibling_copy(cycle, h, o).start()
        for o in range(4):
            for h in range(2):
                sibling_copy(cycle, h, o).wait_recv()

    def collect_end(cycle):
        for h in range(2):
            for o in (1, 2, 3):
                for stage in range(3):
                    gather_copy(cycle, h, stage, o).wait_send()
            for o in range(4):
                sibling_copy(cycle, h, o).wait_send()

    def coarse_product(blocks, state):
        total = blocks[pl.ds(0, 8), :] * state[0:1, :]
        for j in range(1, 8):
            total = total + blocks[pl.ds(8 * j, 8), :] * state[j : j + 1, :]
        return total

    def coupled(cycle):
        links = coarse_links[...]
        lanes, chunks = [], []
        for f in range(6):
            for h in range(2):
                part = jnp.broadcast_to(links[f : f + 1, h * 128 : h * 128 + 128], (8, 128))
                lanes.append(part % 128)
                chunks.append(part // 128)

        def device_step(n, found):
            c, z, y, x = n // 64, n // 16 % 4, n // 4 % 4, n % 4
            number = (((z % 2) * 2 + c) * 32 + y * 8 + x * 2 + z // 2) * 2
            for h in range(2):
                values = held[cycle, c, z, y, x, h]
                found = [
                    jnp.where(chunk == number + h, jnp.take_along_axis(values, at, axis=1), now)
                    for chunk, at, now in zip(chunks, lanes, found)
                ]
            return tuple(found)

        found = lax.fori_loop(0, 128, device_step, tuple(jnp.zeros((8, 128), F32) for _ in range(12)))
        weight = coarse_weight[...]
        total = jnp.zeros((8, 256), F32)
        for f in range(6):
            total = total + weight[f : f + 1, :] * jnp.concatenate(found[2 * f : 2 * f + 2], axis=1)
        return total

    def coarse(cycle, slot):
        left = jnp.concatenate([mt_hi, mt_hi, mt_lo], axis=1)
        for pair in range(8):
            both = [split(dm[pl.ds((2 * pair + h) * 64, 64), :]) for h in range(2)]
            highs = jnp.concatenate([both[0][0], both[1][0]], axis=1)
            lows = jnp.concatenate([both[0][1], both[1][1]], axis=1)
            projected = bf16_dot(left, jnp.concatenate([highs, lows, highs], axis=0))
            p_hi, p_lo = split(projected)
            pj[:, pl.ds(pair * 256, 256)] = jnp.concatenate([p_hi, p_lo], axis=0)
        summed = bf16_dot(pj[...], mem[...])
        restricted = summed[0:8] + summed[8:16]
        state = damping * coarse_product(inv_t, restricted)
        collect(cycle, state)
        applied = coarse_product(diag_t, state) - coupled(cycle)
        state = state + damping * coarse_product(inv_t, restricted - applied)
        s_hi, s_lo = split(exact_dot(modes, state))
        stacked = jnp.concatenate([s_hi, s_lo], axis=0)
        for pair in range(8):
            both = bf16_dot(stacked, mem_t[:, pl.ds(pair * 256, 256)])
            spread = both[0:64] + both[64:128]
            for h in range(2):
                rows = pl.ds((2 * pair + h) * 64, 64)
                wm[rows, :] = wm[rows, :] + spread[:, h * 128 : h * 128 + 128]
        send_x(slot)
        send_y(slot)
        send_z(slot)
        collect_end(cycle)

    for d in range(64):
        rb[d] = rhs[pl.ds(d * 16, 16), :].astype(BF16)
    sweep(0, True)

    @pl.loop(0, 9)
    def _(t):
        slot = t % 2
        operate(slot)

        @pl.when(t % 5 == 1)
        def _():
            coarse(t // 5, 1 - slot)

        @pl.when(t % 5 != 1)
        def _():
            for d in range(64):
                rb[d] = dm[pl.ds(d, 16, stride=64), :].astype(BF16)
            sweep(1 - slot, False)

    operate(1)
    for xy in range(16):
        sol_out[pl.ds(xy, 64, stride=16), :] = wm[pl.ds(xy * 64, 64), :]
        res_out[pl.ds(xy, 64, stride=16), :] = dm[pl.ds(xy * 64, 64), :]


def on_device(
    right_side, mass_coef, conductivity, block_inverse, mass_ref, stiff_ref, face_mass, coarse_modes, elem_agg,
    coarse_diag, coarse_inv, coarse_weight, coarse_links,
):
    vmem = pl.BlockSpec(memory_space=pltpu.VMEM)
    far = pl.BlockSpec(memory_space=pltpu.HBM)
    dma = pltpu.SemaphoreType.DMA
    shape = right_side.shape
    flat = jax.ShapeDtypeStruct((1024, 128), F32)
    solution_now, residual = pl.pallas_call(
        kernel,
        out_shape=(flat, flat),
        in_specs=[far] * 13,
        out_specs=(vmem, vmem),
        scratch_shapes=[
            pltpu.VMEM((1024, 128), F32),
            pltpu.VMEM((16, 128), F32),
            pltpu.VMEM((16, 128), F32),
            pltpu.VMEM((64, 64), F32),
            pltpu.VMEM((64, 64), F32),
            pltpu.VMEM((16, 16), F32),
            pltpu.VMEM((8, 64), F32),
            pltpu.VMEM((16, 128), jnp.int32),
            pltpu.VMEM((64, 256), F32),
            pltpu.VMEM((64, 256), F32),
            pltpu.VMEM((6, 256), F32),
            pltpu.VMEM((6, 256), jnp.int32),
            pltpu.VMEM((64, 64, 16, 128), BF16),
            pltpu.VMEM((1024, 128), F32),
            pltpu.VMEM((1024, 128), F32),
            pltpu.VMEM((1024, 128), F32),
            pltpu.VMEM((64, 16, 128), BF16),
            pltpu.VMEM((64, 256), F32),
            pltpu.VMEM((64, 256), F32),
            pltpu.VMEM((8, 256, 256), BF16),
            pltpu.VMEM((8, 256, 256), BF16),
            pltpu.VMEM((128, 256), BF16),
            pltpu.VMEM((8, 16, 128), F32),
            pltpu.VMEM((2048, 256), BF16),
            pltpu.VMEM((256, 2048), BF16),
            pltpu.VMEM((16, 2048), BF16),
            pltpu.VMEM((2, 4, 64, 128), F32),
            pltpu.VMEM((2, 2, 16, 128), F32),
            pltpu.VMEM((4, 64, 128), F32),
            pltpu.VMEM((2, 16, 128), F32),
            pltpu.VMEM((6, 16, 128), F32),
            pltpu.VMEM((2, 2, 4, 4, 4, 2, 8, 128), F32),
            dma((12,)),
            dma((16,)),
            dma((6,)),
            dma((6,)),
            dma((6,)),
            dma((2, 6)),
            dma((2, 2, 3, 3)),
            dma((2, 2, 3, 3)),
            dma((2, 2, 4)),
            dma((2, 2, 4)),
        ],
        compiler_params=pltpu.CompilerParams(
            collective_id=0, has_side_effects=True, vmem_limit_bytes=63 * 1024 * 1024
        ),
    )(
        right_side.reshape(1024, 128),
        mass_coef.reshape(16, 128),
        conductivity.reshape(16, 128),
        block_inverse.reshape(64, 64, 16, 128),
        mass_ref,
        stiff_ref,
        face_mass,
        coarse_modes.T,
        elem_agg.reshape(16, 128),
        coarse_diag.reshape(64, 256),
        coarse_inv.reshape(64, 256),
        coarse_weight,
        coarse_links,
    )
    return solution_now.reshape(shape), residual.reshape(shape)


def solution(mesh):
    split_all = ("gx", "gy", "gz")
    return jax.shard_map(
        on_device,
        mesh=mesh,
        in_specs=(
            P(None, None, None, "gx", "gy", "gz"),
            P("gx", "gy", "gz"),
            P("gx", "gy", "gz"),
            P(None, None, "gx", "gy", "gz"),
            P(),
            P(),
            P(),
            P(),
            P("gx", "gy", "gz"),
            P(None, None, split_all),
            P(None, None, split_all),
            P(None, split_all),
            P(None, split_all),
        ),
        out_specs=(P(None, None, None, "gx", "gy", "gz"), P(None, None, None, "gx", "gy", "gz")),
        check_vma=False,
    )
```

```python
import functools

import jax
import jax.numpy as jnp
from jax import lax
from jax.experimental import pallas as pl
from jax.experimental.pallas import tpu as pltpu
from jax.sharding import PartitionSpec as P

MESH = pl.DeviceIdType.MESH
F32 = jnp.float32
BF16 = jnp.bfloat16
damping = 0.8

XL, XU, YL, YU, ZL, ZU = range(6)
ROW_MASS, ROW_STIFF, ROW_XL, ROW_XU, ROW_YL, ROW_YU, ROW_ZL, ROW_ZU = 0, 64, 128, 160, 192, 208, 224, 240


DOF_STEP, ELEMENT_STEP = 49, 3


def of_element(xy, first=0, count=64):
    return pl.ds(DOF_STEP * first + ELEMENT_STEP * xy, count, stride=DOF_STEP)


def of_dof(k, q):
    return pl.ds(DOF_STEP * (16 * k + q), 16, stride=ELEMENT_STEP)


def exact_dot(a, b, dims=(((1,), (0,)), ((), ()))):
    return lax.dot_general(a, b, dims, precision=lax.Precision.HIGHEST, preferred_element_type=F32)


def bf16_dot(a, b):
    return lax.dot_general(a, b, (((1,), (0,)), ((), ())), preferred_element_type=F32)


def split(value):
    high = value.astype(BF16)
    return high, (value - high.astype(F32)).astype(BF16)


def iota(shape, dim):
    return lax.broadcasted_iota(jnp.int32, shape, dim)


def row_of(dof):
    return dof % 4 * 16 + dof // 4


def stacked_operator(mass_ref, stiff_ref, face_mass):
    ordered = (iota((64, 64), 0) == row_of(iota((64, 64), 1))).astype(F32)
    dof, col = iota((64, 256), 0), iota((64, 256), 1)
    total = exact_dot(exact_dot(ordered, mass_ref), (col == row_of(dof) + ROW_MASS).astype(F32))
    total = total + exact_dot(exact_dot(ordered, stiff_ref), (col == row_of(dof) + ROW_STIFF).astype(F32))
    r, q = iota((64, 16), 0), iota((64, 16), 1)
    c, col = iota((16, 256), 0), iota((16, 256), 1)
    q_hi, q_lo = q // 4, q % 4
    c_hi, c_lo = c // 4, c % 4
    faces = (
        (16 * q_lo + q_hi, ROW_XL + c_lo * 8 + 4 + c_hi),
        (16 * q_lo + 12 + q_hi, ROW_XU + c_lo * 8 + c_hi),
        (16 * q_lo + 4 * q_hi, ROW_YL + 4 * c_lo + c_hi),
        (16 * q_lo + 4 * q_hi + 3, ROW_YU + 4 * c_lo + c_hi),
        (q, ROW_ZL + c),
        (48 + q, ROW_ZU + c),
    )
    for target, source in faces:
        placed = exact_dot((r == target).astype(F32), face_mass)
        total = total - exact_dot(placed, (col == source).astype(F32))
    return total


def kernel(
    rhs_in, mass_coef_in, kappa_in, block_inverse, mass_ref_in, stiff_ref_in, face_mass_in, modes_t_in, elem_agg_in,
    coarse_diag_in, coarse_inv_in, coarse_weight_in, coarse_links_in,
    sol_out, res_out,
    rhs, mass_coef, kappa, mass_ref, stiff_ref, face_mass, modes_t, elem_agg,
    coarse_diag, coarse_inv, coarse_weight, coarse_links,
    bvm, wm, dm, td, tw, rhsm, rb, diag_t, inv_t, zhi, zlo, whl, wf, wz, coef_z, coef, mem, mem_t, picked, chunk_of, pj, rx, rz, sx, sz, krecv, held, leaving, out_sem,
    in_sem, b_sem, k_send, k_recv, h_send, h_recv, p_send, p_recv, g_send, g_recv, d_send, d_recv,
):
    gx, gy, gz = lax.axis_index("gx"), lax.axis_index("gy"), lax.axis_index("gz")
    core = gx % 2
    place = (gz // 2, gy, (gz % 2) * 2 + gx // 2)

    def device(chip, which):
        return ((chip[2] % 2) * 2 + which, chip[1], chip[0] * 2 + chip[2] // 2)

    def moved(dim, offset, other=None, more=0):
        by = {dim: offset, other: more}
        return tuple((v + by[d]) % 4 if d in by else v for d, v in enumerate(place))

    beside = (
        ((gx + 3) % 4, gy, gz), ((gx + 1) % 4, gy, gz),
        (gx, (gy + 3) % 4, gz), (gx, (gy + 1) % 4, gz),
        (gx, gy, (gz + 7) % 8), (gx, gy, (gz + 1) % 8),
    )
    sibling = device(place, 1 - core)
    routes = ((0, 1, 2), (1, 2, 0))
    steps = tuple((a, b) for a in range(4) for b in range(4) if a or b)
    plane = [[device(moved(r[0], a, r[1], b), core) for a, b in steps] for r in routes]
    line = [[device(moved(r[2], o), core) for o in (1, 2, 3)] for r in routes]

    def block_copy(n):
        rows = pl.ds(8 * n, 8)
        return pltpu.make_async_copy(block_inverse.at[rows], bvm.at[rows], b_sem.at[n])

    arriving = [
        pltpu.make_async_copy(src, dst, in_sem.at[n])
        for n, (src, dst) in enumerate(
            (
                (kappa_in, kappa), (rhs_in, rhs), (mass_ref_in, mass_ref), (stiff_ref_in, stiff_ref),
                (face_mass_in, face_mass), (modes_t_in, modes_t), (elem_agg_in, elem_agg), (mass_coef_in, mass_coef),
                (coarse_diag_in, coarse_diag), (coarse_inv_in, coarse_inv),
                (coarse_weight_in, coarse_weight), (coarse_links_in, coarse_links),
            )
        )
    ]
    for copy in arriving:
        copy.start()
    for n in range(8):
        block_copy(n).start()

    barrier = pltpu.get_barrier_semaphore()
    greeted = list(beside) + [sibling] + plane[0] + plane[1]
    for target in greeted:
        pl.semaphore_signal(barrier, inc=1, device_id=target, device_id_type=MESH)
    pl.semaphore_wait(barrier, len(greeted))

    def remote(src, dst, send, recv, target):
        return pltpu.make_async_remote_copy(
            src_ref=src, dst_ref=dst, send_sem=send, recv_sem=recv, device_id=target, device_id_type=MESH
        )

    exists = (gx > 0, gx < 3, gy > 0, gy < 3, gz > 0, gz < 7)

    def kappa_copy(f):
        return remote(kappa, krecv.at[f ^ 1], k_send.at[f], k_recv.at[f ^ 1], beside[f])

    arriving[0].wait()
    for f in range(6):
        pl.when(exists[f])(lambda: kappa_copy(f).start())

        @pl.when(jnp.logical_not(exists[f]))
        def _():
            krecv[f] = jnp.zeros((16, 128), F32)
            for slot in range(2):
                if f < 4:
                    rx[slot, f] = jnp.zeros((64, 128), F32)
                else:
                    rz[slot, f - 4] = jnp.zeros((16, 128), F32)

    arriving[1].wait()
    wm[...] = jnp.zeros_like(wm)
    for d in range(64):
        part = rhs[pl.ds(d * 16, 16), :]
        td[of_dof(d % 4, d // 4), :] = part
        rb[d] = part.astype(BF16)

    half = iota((8, 128), 0) < 4
    lane16 = iota((16, 128), 1)

    def face_copy(f, slot):
        if f < 4:
            src, dst = sx.at[f], rx.at[slot, f ^ 1]
        else:
            src, dst = sz.at[f - 4], rz.at[slot, (f ^ 1) - 4]
        return remote(src, dst, h_send.at[f], h_recv.at[slot, f ^ 1], beside[f])

    def send(f, slot):
        pl.when(exists[f])(lambda: face_copy(f, slot).start())

    def send_x(slot):
        for y in range(4):
            for pair in range(2):
                at = pl.ds(y * 16 + pair * 8, 8)
                low, up = y * 64 + 32 * pair, (12 + y) * 64 + 32 * pair + 8
                sx[XL, at, :] = jnp.where(half, wm[pl.ds(low, 8), :], pltpu.roll(wm[pl.ds(low + 16, 8), :], 4, 0))
                sx[XU, at, :] = jnp.where(half, pltpu.roll(wm[pl.ds(up, 8), :], 4, 0), wm[pl.ds(up + 16, 8), :])
        send(XL, slot)
        send(XU, slot)

    def send_y(slot):
        for x in range(4):
            at = pl.ds(x * 16, 16)
            sx[YL, at, :] = wm[pl.ds(4 * x * 64, 16, stride=4), :]
            sx[YU, at, :] = wm[pl.ds((4 * x + 3) * 64 + 3, 16, stride=4), :]
        send(YL, slot)
        send(YU, slot)

    def send_z(slot):
        lower = upper = jnp.zeros((16, 128), F32)
        for xy in range(16):
            lower = jnp.where(lane16 == xy, pltpu.roll(wm[pl.ds(xy * 64, 16), :], xy, 1), lower)
            upper = jnp.where(lane16 == xy, pltpu.roll(wm[pl.ds(xy * 64 + 48, 16), :], xy + 1, 1), upper)
        sz[0] = lower
        sz[1] = upper
        send(ZL, slot)
        send(ZU, slot)

    def spot(xy):
        x, y = xy // 4, xy % 4
        return (2 * x, y - 1) if y in (1, 2) else (2 * x + 1, y // 3)

    def operate(slot):
        def put(xy, at, count, which, value):
            pair, h = spot(xy)
            lanes = pl.ds(h * 128, 128)
            value = coef[which, pl.ds(xy, 1), :] * value
            high = value.astype(BF16)
            zhi[pair, pl.ds(at, count), lanes] = high
            zlo[pair, pl.ds(at, count), lanes] = (value - high.astype(F32)).astype(BF16)

        for xy in range(16):
            x, y = xy // 4, xy % 4
            here = wm[pl.ds(xy * 64, 64), :]
            put(xy, ROW_MASS, 64, 0, here)
            put(xy, ROW_STIFF, 64, 1, here)
            if x > 0:
                low = [wm[pl.ds((xy - 4) * 64 + 16 * k + 8, 8), :] for k in range(4)]
                put(xy, ROW_XL, 32, 2, jnp.concatenate(low, axis=0))
            if x < 3:
                up = [wm[pl.ds((xy + 4) * 64 + 16 * k, 8), :] for k in range(4)]
                put(xy, ROW_XU, 32, 3, jnp.concatenate(up, axis=0))
            if y > 0:
                put(xy, ROW_YL, 16, 4, wm[pl.ds((xy - 1) * 64 + 3, 16, stride=4), :])
            if y < 3:
                put(xy, ROW_YU, 16, 5, wm[pl.ds((xy + 1) * 64, 16, stride=4), :])

        def arrived(*places):
            for f in places:

                @pl.when(exists[f])
                def _():
                    face_copy(f, slot).wait_send()
                    face_copy(f ^ 1, slot).wait_recv()

        def store(xy, left, last):
            dm[pl.ds(xy * 64, 64), :] = left
            if last:
                td[of_element(xy), :] = left

        def apply(pair):
            both = bf16_dot(whl[...], zhi[pair])
            applied = both[0:64] + (both[64:128] + bf16_dot(whl[pl.ds(0, 64), :], zlo[pair]))
            for xy in range(16):
                if spot(xy)[0] == pair:
                    h = spot(xy)[1]
                    store(xy, rhsm[pl.ds(xy * 64, 64), :] - applied[:, h * 128 : h * 128 + 128], False)

        def from_beside(f, elements, last):
            parts = [
                split(coef[2 + f, pl.ds(xy, 1), :] * rx[slot, f, pl.ds((xy % 4 if f < 2 else xy // 4) * 16, 16), :])
                for xy in elements
            ]
            high, low = (jnp.concatenate([parts[0][n], parts[1][n]], axis=1) for n in range(2))
            added = bf16_dot(wf[f], jnp.concatenate([high, low, high, high], axis=0))
            for h, xy in enumerate(elements):
                store(xy, dm[pl.ds(xy * 64, 64), :] - added[:, h * 128 : h * 128 + 128], last)

        for xy in range(16):
            below = pltpu.roll(wm[pl.ds(xy * 64 + 48, 16), :], 1, 1)
            above = pltpu.roll(wm[pl.ds(xy * 64, 16), :], 127, 1)
            put(xy, ROW_ZL, 16, 6, jnp.where(lane16 == 0, 0.0, below))
            put(xy, ROW_ZU, 16, 7, jnp.where(lane16 == 127, 0.0, above))
        for pair in range(8):
            apply(pair)
        arrived(ZL, ZU)
        for n, first, lane in ((0, 0, 0), (1, 48, 127)):
            high, low = split(coef_z[pl.ds(n, 1), :] * rz[slot, n])
            added = bf16_dot(wz[...], jnp.concatenate([high, low, high, high], axis=0))
            for xy in range(16):
                rows = pl.ds(xy * 64 + first, 16)
                at_lane = jnp.where(lane16 == lane, pltpu.roll(added, (lane - xy) % 128, 1), 0.0)
                dm[rows, :] = dm[rows, :] - at_lane
        for xy in (5, 6, 9, 10):
            td[of_element(xy), :] = dm[pl.ds(xy * 64, 64), :]
        arrived(XL, XU)
        for f, at in ((XL, 0), (XU, 12)):
            from_beside(f, (at + 1, at + 2), True)
            from_beside(f, (at, at + 3), False)
        arrived(YL, YU)
        for f, at in ((YL, 0), (YU, 3)):
            from_beside(f, (at, at + 4), True)
            from_beside(f, (at + 8, at + 12), True)

    adder = (iota((16, 256), 1) % 16 == iota((16, 256), 0)).astype(F32).astype(BF16)

    def block_rows(dofs):
        groups = [[], [], [], []]
        for g in range(16):
            column = [rb[4 * g + j] for j in range(4)]
            for i, (k, q) in enumerate(dofs):
                m = [bvm[4 * q + k, 4 * g + j] * column[j] for j in range(4)]
                groups[i].append((m[0] + m[1]) + (m[2] + m[3]))
        rows = [jnp.concatenate(g, axis=0) for g in groups]
        for pair in range(2):
            sums = bf16_dot(adder, jnp.concatenate(rows[2 * pair : 2 * pair + 2], axis=1))
            for i in range(2):
                k, q = dofs[2 * pair + i]
                tw[of_dof(k, q), :] = damping * sums[:, 128 * i : 128 * i + 128]

    def outer(n):
        block_rows([(0, 2 * n), (3, 2 * n), (0, 2 * n + 1), (3, 2 * n + 1)])

    def middle(q, r):
        block_rows([(1, q), (2, q), (1, r), (2, r)])

    def add_update(first, count):
        for xy in range(16):
            rows = pl.ds(xy * 64 + first, count)
            wm[rows, :] = wm[rows, :] + tw[of_element(xy, first, count), :]

    def sweep(slot):
        pl.loop(0, 8)(outer)
        add_update(0, 16)
        add_update(48, 16)
        send_z(slot)
        pl.loop(0, 4)(lambda n: middle(2 * n + 8 * (n // 2), 2 * n + 8 * (n // 2) + 1))
        pl.loop(0, 2)(lambda n: middle(4 + 4 * n, 7 + 4 * n))
        for k in (1, 2):
            for q in (5, 6, 9, 10):
                tw[of_dof(k, q), :] = jnp.zeros((16, 128), F32)
        add_update(16, 32)
        send_x(slot)
        send_y(slot)
        pl.loop(0, 2)(lambda n: middle(5 + 4 * n, 6 + 4 * n))
        sub = iota((8, 128), 0)
        off_face = ((sub == 5) | (sub == 6), (sub == 1) | (sub == 2))
        for xy in range(16):
            for v in range(4):
                rows = pl.ds(xy * 64 + 16 + 8 * v, 8)
                wm[rows, :] = wm[rows, :] + jnp.where(off_face[v % 2], tw[of_element(xy, 16 + 8 * v, 8), :], 0.0)

    def first_sweep(slot):
        @pl.loop(0, 8)
        def _(n):
            block_copy(n).wait()
            outer(n)
            middle(2 * n, 2 * n + 1)

        add_update(0, 64)
        send_z(slot)
        send_x(slot)
        send_y(slot)

    first_sweep(0)

    for copy in arriving[2:]:
        copy.wait()

    for xy in range(16):
        rhsm[pl.ds(xy * 64, 64), :] = td[of_element(xy), :]
    high, low = split(stacked_operator(mass_ref[...], stiff_ref[...], face_mass[...]))
    whl[pl.ds(0, 64), :] = high
    whl[pl.ds(64, 64), :] = low
    col = iota((256, 256), 1)
    face, part, c = col // 64, col % 64 // 16, col % 16
    along_x = jnp.where(face == 0, ROW_XL + 4, ROW_XU) + c // 4 * 8 + c % 4
    along_y = jnp.where(face == 2, ROW_YL, ROW_YU) + c
    chosen = iota((256, 256), 0) == jnp.where(face < 2, along_x, along_y)
    taken = bf16_dot(high, (chosen & (part < 2)).astype(F32).astype(BF16))
    taken = taken + bf16_dot(low, (chosen & (part == 2)).astype(F32).astype(BF16))
    for f in range(4):
        wf[f] = taken[:, 64 * f : 64 * f + 64].astype(BF16)
    col = iota((256, 64), 1)
    part, chosen = col // 16, iota((256, 64), 0) == ROW_ZL + col % 16
    taken = bf16_dot(high[0:16], (chosen & (part < 2)).astype(F32).astype(BF16))
    taken = taken + bf16_dot(low[0:16], (chosen & (part == 2)).astype(F32).astype(BF16))
    wz[...] = taken.astype(BF16)
    zhi[...] = jnp.zeros_like(zhi)
    zlo[...] = jnp.zeros_like(zlo)
    ordered = (iota((64, 64), 0) == row_of(iota((64, 64), 1))).astype(F32)
    modes = exact_dot(ordered, modes_t[...], (((1,), (1,)), ((), ())))
    mt_hi, mt_lo = split(exact_dot(modes_t[...], ordered, (((1,), (1,)), ((), ()))))
    for f in range(6):

        @pl.when(exists[f])
        def _():
            kappa_copy(f).wait_send()
            kappa_copy(f ^ 1).wait_recv()

    own = kappa[...]
    row, lane = iota((16, 128), 0), iota((16, 128), 1)
    down_x = jnp.concatenate([krecv[XL][12:16], own[0:12]], axis=0)
    up_x = jnp.concatenate([own[4:16], krecv[XU][0:4]], axis=0)
    down_y = jnp.where(row % 4 == 0, jnp.roll(krecv[YL], -3, 0), jnp.roll(own, 1, 0))
    up_y = jnp.where(row % 4 == 3, jnp.roll(krecv[YU], 3, 0), jnp.roll(own, -1, 0))
    down_z = jnp.where(lane == 0, pltpu.roll(krecv[ZL], 1, 1), pltpu.roll(own, 1, 1))
    up_z = jnp.where(lane == 127, pltpu.roll(krecv[ZU], 127, 1), pltpu.roll(own, 127, 1))
    outside = (
        (row < 4) & (gx == 0), (row >= 12) & (gx == 3),
        (row % 4 == 0) & (gy == 0), (row % 4 == 3) & (gy == 3),
        (lane == 0) & (gz == 0), (lane == 127) & (gz == 7),
    )
    coef[0] = mass_coef[...]
    coef[1] = own
    for f, near in enumerate((down_x, up_x, down_y, up_y, down_z, up_z)):
        near = jnp.where(outside[f], 0.0, near)
        coef[2 + f] = 2.0 * own * near / (own + near)
    here = (row == lane).astype(F32)
    coef_z[0:1, :] = jnp.sum(here * coef[6][:, 0:1], axis=0, keepdims=True)
    coef_z[1:2, :] = jnp.sum(here * coef[7][:, 127:128], axis=0, keepdims=True)

    def coarse_setup():
        turned = (iota((64, 64), 1) == iota((64, 64), 0) % 8 * 8 + iota((64, 64), 0) // 8).astype(F32)
        inv_t[...] = exact_dot(turned, coarse_inv[...])
        diag_t[...] = exact_dot(turned, coarse_diag[...])
        agg = elem_agg[...]
        eye128 = (iota((128, 128), 0) == iota((128, 128), 1)).astype(F32)
        agg_t = exact_dot(eye128, agg.astype(F32), (((1,), (1,)), ((), ())))
        links = coarse_links[...]
        for f in range(4):
            picked[f] = ((links[f : f + 1, :] & 127) == (iota((256, 256), 0) & 127)).astype(F32).astype(BF16)
        for f in range(6):
            chunk_of[f] = jnp.broadcast_to(links[f : f + 1, :] >> 7, (8, 256))
        numbers = iota((128, 256), 1).astype(F32)
        for xy in range(16):
            mem[pl.ds(xy * 128, 128), :] = (agg_t[:, xy : xy + 1] == numbers).astype(F32).astype(BF16)

    def whole(cycle, half_id, which, done, chip):
        index = [slice(None) if d in done else chip[d] for d in range(3)]
        return held.at[cycle, which, index[2], index[1], index[0], half_id]

    def plane_copy(cycle, half_id, n):
        block = whole(cycle, half_id, core, (), place)
        at = (cycle, half_id, n)
        return remote(block, block, p_send.at[at], p_recv.at[at], plane[half_id][n])

    def line_copy(cycle, half_id, o):
        block = whole(cycle, half_id, core, routes[half_id][:2], place)
        at = (cycle, half_id, o - 1)
        return remote(block, block, g_send.at[at], g_recv.at[at], line[half_id][o - 1])

    def sibling_copy(cycle, half_id, o):
        route = routes[half_id]
        chip = moved(route[2], -o)
        block = whole(cycle, half_id, core, route[:2], chip)
        at = (cycle, half_id, o)
        return remote(block, block, d_send.at[at], d_recv.at[at], sibling)

    def collect(cycle, state):
        for h in range(2):
            held[cycle, core, place[2], place[1], place[0], h] = state[:, h * 128 : h * 128 + 128]

        for n in range(15):
            for h in range(2):
                plane_copy(cycle, h, n).start()
        numbers_t = iota((256, 128), 0)
        for xy in range(16):
            mem_t[:, pl.ds(xy * 128, 128)] = (elem_agg[pl.ds(xy, 1), :] == numbers_t).astype(F32).astype(BF16)
        for h in range(2):
            for n in range(15):
                plane_copy(cycle, h, n).wait_recv()
            for o in (1, 2, 3):
                line_copy(cycle, h, o).start()
        for h in range(2):
            sibling_copy(cycle, h, 0).start()

        lanes = [
            jnp.broadcast_to(coarse_links[f : f + 1, h * 128 : h * 128 + 128] & 127, (8, 128)) for f in (4, 5) for h in range(2)
        ]
        chunks = [chunk_of[f, :, h * 128 : h * 128 + 128] for f in range(6) for h in range(2)]

        def look(found, which, o):
            numbers, values = [], []
            for half_id in range(2):
                route = routes[half_id]
                chip = moved(route[2], -o)
                for n in range(16):
                    x, y, z = (n // 4 if d == route[0] else n % 4 if d == route[1] else chip[d] for d in range(3))
                    numbers.append((((z % 2) * 2 + which) * 32 + y * 8 + x * 2 + z // 2) * 2 + half_id)
                    values.append(held[cycle, which, z, y, x, half_id])
            lhs = jnp.concatenate(split(jnp.concatenate(values, axis=0)), axis=1)
            found = list(found)
            for f in range(6):
                at_lane = bf16_dot(lhs, picked[f]) if f < 4 else None
                for h in range(2):
                    for n in range(32):
                        if f < 4:
                            value = at_lane[8 * n : 8 * n + 8, 128 * h : 128 * h + 128]
                        else:
                            value = jnp.take_along_axis(values[n], lanes[2 * f + h - 8], axis=1)
                        found[2 * f + h] = jnp.where(chunks[2 * f + h] == numbers[n], value, found[2 * f + h])
            return found

        found = look([jnp.zeros((8, 128), F32) for _ in range(12)], core, 0)
        for h in range(2):
            sibling_copy(cycle, h, 0).wait_recv()
        found = look(found, 1 - core, 0)
        for o in (1, 3, 2):
            for h in range(2):
                line_copy(cycle, h, o).wait_recv()
                sibling_copy(cycle, h, o).start()
            found = look(found, core, o)
        for o in (1, 3, 2):
            for h in range(2):
                sibling_copy(cycle, h, o).wait_recv()
            found = look(found, 1 - core, o)
        weight = coarse_weight[...]
        total = jnp.zeros((8, 256), F32)
        for f in range(6):
            total = total + weight[f : f + 1, :] * jnp.concatenate(found[2 * f : 2 * f + 2], axis=1)
        return total

    def collect_end(cycle):
        for h in range(2):
            for n in range(15):
                plane_copy(cycle, h, n).wait_send()
            for o in (1, 2, 3):
                line_copy(cycle, h, o).wait_send()
            for o in range(4):
                sibling_copy(cycle, h, o).wait_send()

    def coarse_product(blocks, state):
        total = blocks[pl.ds(0, 8), :] * state[0:1, :]
        for j in range(1, 8):
            total = total + blocks[pl.ds(8 * j, 8), :] * state[j : j + 1, :]
        return total

    def coarse(cycle, slot):
        left = jnp.concatenate([mt_hi, mt_hi, mt_lo], axis=1)
        for pair in range(8):
            both = [split(dm[pl.ds((2 * pair + h) * 64, 64), :]) for h in range(2)]
            highs = jnp.concatenate([both[0][0], both[1][0]], axis=1)
            lows = jnp.concatenate([both[0][1], both[1][1]], axis=1)
            projected = bf16_dot(left, jnp.concatenate([highs, lows, highs], axis=0))
            p_hi, p_lo = split(projected)
            pj[:, pl.ds(pair * 256, 256)] = jnp.concatenate([p_hi, p_lo], axis=0)
        summed = bf16_dot(pj[...], mem[...])
        restricted = summed[0:8] + summed[8:16]
        state = damping * coarse_product(inv_t, restricted)
        applied = coarse_product(diag_t, state) - collect(cycle, state)
        state = state + damping * coarse_product(inv_t, restricted - applied)
        s_hi, s_lo = split(exact_dot(modes, state))
        stacked = jnp.concatenate([s_hi, s_lo], axis=0)
        for pair in range(8):
            both = bf16_dot(stacked, mem_t[:, pl.ds(pair * 256, 256)])
            spread = both[0:64] + both[64:128]
            for h in range(2):
                rows = pl.ds((2 * pair + h) * 64, 64)
                wm[rows, :] = wm[rows, :] + spread[:, h * 128 : h * 128 + 128]
        send_z(slot)
        send_x(slot)
        send_y(slot)
        collect_end(cycle)

    @pl.loop(0, 9)
    def _(t):
        slot = t % 2
        operate(slot)

        @pl.when(t % 5 == 1)
        def _():
            coarse(t // 5, 1 - slot)

        @pl.when(t % 5 != 1)
        def _():
            for d in range(64):
                rb[d] = td[of_dof(d % 4, d // 4), :].astype(BF16)
            sweep(1 - slot)
            pl.when(t == 0)(coarse_setup)

    def leave(n, source, target):
        for d in range(64):
            leaving[n, pl.ds(d * 16, 16), :] = source[of_dof(d % 4, d // 4), :]
        return pltpu.make_async_copy(leaving.at[n], target, out_sem.at[n])

    for xy in range(16):
        tw[of_element(xy), :] = wm[pl.ds(xy * 64, 64), :]
    first_out = leave(0, tw, sol_out)
    first_out.start()
    operate(1)
    second_out = leave(1, td, res_out)
    second_out.start()
    first_out.wait()
    second_out.wait()


def write_out(first, second, first_out, second_out, held, in_sems, out_sems):
    parts = [(m, pl.ds(n * 256, 256), n) for m in range(2) for n in range(4)]
    ends = ((first, first_out), (second, second_out))
    into = [pltpu.make_async_copy(ends[m][0].at[at], held.at[m, at], in_sems.at[m, n]) for m, at, n in parts]
    out = [pltpu.make_async_copy(held.at[m, at], ends[m][1].at[at], out_sems.at[m, n]) for m, at, n in parts]
    for copy in into:
        copy.start()
    for arriving, leaving in zip(into, out):
        arriving.wait()
        leaving.start()
    for copy in out:
        copy.wait()


def on_device(
    right_side, mass_coef, conductivity, block_inverse, mass_ref, stiff_ref, face_mass, coarse_modes, elem_agg,
    coarse_diag, coarse_inv, coarse_weight, coarse_links,
):
    far = pl.BlockSpec(memory_space=pltpu.HBM)
    dma = pltpu.SemaphoreType.DMA
    shape = right_side.shape
    flat = jax.ShapeDtypeStruct((1024, 128), F32)
    solution_now, residual = pl.pallas_call(
        kernel,
        out_shape=(flat, flat),
        in_specs=[far] * 13,
        out_specs=(far, far),
        scratch_shapes=[
            pltpu.VMEM((1024, 128), F32),
            pltpu.VMEM((16, 128), F32),
            pltpu.VMEM((16, 128), F32),
            pltpu.VMEM((64, 64), F32),
            pltpu.VMEM((64, 64), F32),
            pltpu.VMEM((16, 16), F32),
            pltpu.VMEM((8, 64), F32),
            pltpu.VMEM((16, 128), jnp.int32),
            pltpu.VMEM((64, 256), F32),
            pltpu.VMEM((64, 256), F32),
            pltpu.VMEM((6, 256), F32),
            pltpu.VMEM((6, 256), jnp.int32),
            pltpu.VMEM((64, 64, 16, 128), BF16),
            pltpu.VMEM((1024, 128), F32),
            pltpu.VMEM((1024, 128), F32),
            pltpu.VMEM((64 * DOF_STEP, 128), F32),
            pltpu.VMEM((64 * DOF_STEP, 128), F32),
            pltpu.VMEM((1024, 128), F32),
            pltpu.VMEM((64, 16, 128), BF16),
            pltpu.VMEM((64, 256), F32),
            pltpu.VMEM((64, 256), F32),
            pltpu.VMEM((8, 256, 256), BF16),
            pltpu.VMEM((8, 256, 256), BF16),
            pltpu.VMEM((128, 256), BF16),
            pltpu.VMEM((4, 64, 64), BF16),
            pltpu.VMEM((16, 64), BF16),
            pltpu.VMEM((2, 128), F32),
            pltpu.VMEM((8, 16, 128), F32),
            pltpu.VMEM((2048, 256), BF16),
            pltpu.VMEM((256, 2048), BF16),
            pltpu.VMEM((4, 256, 256), BF16),
            pltpu.VMEM((6, 8, 256), jnp.int32),
            pltpu.VMEM((16, 2048), BF16),
            pltpu.VMEM((2, 4, 64, 128), F32),
            pltpu.VMEM((2, 2, 16, 128), F32),
            pltpu.VMEM((4, 64, 128), F32),
            pltpu.VMEM((2, 16, 128), F32),
            pltpu.VMEM((6, 16, 128), F32),
            pltpu.VMEM((2, 2, 4, 4, 4, 2, 8, 128), F32),
            pltpu.VMEM((2, 1024, 128), F32),
            dma((2,)),
            dma((12,)),
            dma((8,)),
            dma((6,)),
            dma((6,)),
            dma((6,)),
            dma((2, 6)),
            dma((2, 2, 15)),
            dma((2, 2, 15)),
            dma((2, 2, 3)),
            dma((2, 2, 3)),
            dma((2, 2, 4)),
            dma((2, 2, 4)),
        ],
        compiler_params=pltpu.CompilerParams(
            collective_id=0, has_side_effects=True, vmem_limit_bytes=63 * 1024 * 1024
        ),
    )(
        right_side.reshape(1024, 128),
        mass_coef.reshape(16, 128),
        conductivity.reshape(16, 128),
        block_inverse.reshape(64, 64, 16, 128),
        mass_ref,
        stiff_ref,
        face_mass,
        coarse_modes.T,
        elem_agg.reshape(16, 128),
        coarse_diag.reshape(64, 256),
        coarse_inv.reshape(64, 256),
        coarse_weight,
        coarse_links,
    )
    solution_now, residual = pl.pallas_call(
        write_out,
        out_shape=(flat, flat),
        in_specs=[far] * 2,
        out_specs=(far, far),
        scratch_shapes=[pltpu.VMEM((2, 1024, 128), F32), dma((2, 4)), dma((2, 4))],
        compiler_params=pltpu.CompilerParams(vmem_limit_bytes=63 * 1024 * 1024),
    )(solution_now, residual)
    return solution_now.reshape(shape), residual.reshape(shape)


def solution(mesh):
    split_all = ("gx", "gy", "gz")
    return jax.shard_map(
        on_device,
        mesh=mesh,
        in_specs=(
            P(None, None, None, "gx", "gy", "gz"),
            P("gx", "gy", "gz"),
            P("gx", "gy", "gz"),
            P(None, None, "gx", "gy", "gz"),
            P(),
            P(),
            P(),
            P(),
            P("gx", "gy", "gz"),
            P(None, None, split_all),
            P(None, None, split_all),
            P(None, split_all),
            P(None, split_all),
        ),
        out_specs=(P(None, None, None, "gx", "gy", "gz"), P(None, None, None, "gx", "gy", "gz")),
        check_vma=False,
    )
```

```python
import functools

import jax
import jax.numpy as jnp
from jax import lax
from jax.experimental import pallas as pl
from jax.experimental.pallas import tpu as pltpu
from jax.sharding import PartitionSpec as P

MESH = pl.DeviceIdType.MESH
F32 = jnp.float32
BF16 = jnp.bfloat16
damping = 0.8

XL, XU, YL, YU, ZL, ZU = range(6)
ROW_MASS, ROW_STIFF, ROW_XL, ROW_XU, ROW_YL, ROW_YU, ROW_ZL, ROW_ZU = 0, 64, 128, 160, 192, 208, 224, 240


DOF_STEP, ELEMENT_STEP = 49, 3


def of_element(xy, first=0, count=64):
    return pl.ds(DOF_STEP * first + ELEMENT_STEP * xy, count, stride=DOF_STEP)


def of_dof(k, q):
    return pl.ds(DOF_STEP * (16 * k + q), 16, stride=ELEMENT_STEP)


def exact_dot(a, b, dims=(((1,), (0,)), ((), ()))):
    return lax.dot_general(a, b, dims, precision=lax.Precision.HIGHEST, preferred_element_type=F32)


def bf16_dot(a, b):
    return lax.dot_general(a, b, (((1,), (0,)), ((), ())), preferred_element_type=F32)


def split(value):
    high = value.astype(BF16)
    return high, (value - high.astype(F32)).astype(BF16)


def iota(shape, dim):
    return lax.broadcasted_iota(jnp.int32, shape, dim)


def row_of(dof):
    return dof % 4 * 16 + dof // 4


def stacked_operator(mass_ref, stiff_ref, face_mass):
    ordered = (iota((64, 64), 0) == row_of(iota((64, 64), 1))).astype(F32)
    dof, col = iota((64, 256), 0), iota((64, 256), 1)
    total = exact_dot(exact_dot(ordered, mass_ref), (col == row_of(dof) + ROW_MASS).astype(F32))
    total = total + exact_dot(exact_dot(ordered, stiff_ref), (col == row_of(dof) + ROW_STIFF).astype(F32))
    r, q = iota((64, 16), 0), iota((64, 16), 1)
    c, col = iota((16, 256), 0), iota((16, 256), 1)
    q_hi, q_lo = q // 4, q % 4
    c_hi, c_lo = c // 4, c % 4
    faces = (
        (16 * q_lo + q_hi, ROW_XL + c_lo * 8 + 4 + c_hi),
        (16 * q_lo + 12 + q_hi, ROW_XU + c_lo * 8 + c_hi),
        (16 * q_lo + 4 * q_hi, ROW_YL + 4 * c_lo + c_hi),
        (16 * q_lo + 4 * q_hi + 3, ROW_YU + 4 * c_lo + c_hi),
        (q, ROW_ZL + c),
        (48 + q, ROW_ZU + c),
    )
    for target, source in faces:
        placed = exact_dot((r == target).astype(F32), face_mass)
        total = total - exact_dot(placed, (col == source).astype(F32))
    return total


def kernel(
    rhs_in, mass_coef_in, kappa_in, block_inverse, mass_ref_in, stiff_ref_in, face_mass_in, modes_t_in, elem_agg_in,
    coarse_diag_in, coarse_inv_in, coarse_weight_in, coarse_links_in,
    sol_out, res_out,
    rhs, mass_coef, kappa, mass_ref, stiff_ref, face_mass, modes_t, elem_agg,
    coarse_diag, coarse_inv, coarse_weight, coarse_links,
    bvm, wm, dm, td, tw, rhsm, rb, diag_t, inv_t, zhi, zlo, whl, wf, wz, coef_z, coef, mem, mem_t, picked, chunk_of, pj, rx, rz, sx, sz, krecv, held, leaving, out_sem,
    in_sem, b_sem, k_send, k_recv, h_send, h_recv, p_send, p_recv, g_send, g_recv, d_send, d_recv,
):
    gx, gy, gz = lax.axis_index("gx"), lax.axis_index("gy"), lax.axis_index("gz")
    core = gx % 2
    place = (gz // 2, gy, (gz % 2) * 2 + gx // 2)

    def device(chip, which):
        return ((chip[2] % 2) * 2 + which, chip[1], chip[0] * 2 + chip[2] // 2)

    def moved(dim, offset, other=None, more=0):
        by = {dim: offset, other: more}
        return tuple((v + by[d]) % 4 if d in by else v for d, v in enumerate(place))

    beside = (
        ((gx + 3) % 4, gy, gz), ((gx + 1) % 4, gy, gz),
        (gx, (gy + 3) % 4, gz), (gx, (gy + 1) % 4, gz),
        (gx, gy, (gz + 7) % 8), (gx, gy, (gz + 1) % 8),
    )
    sibling = device(place, 1 - core)
    routes = ((0, 1, 2), (1, 2, 0))
    hops = (0, 3, 4, 3)
    steps = sorted(((a, b) for a in range(4) for b in range(4) if a or b), key=lambda s: -hops[s[0]] - hops[s[1]])
    plane = [[device(moved(r[0], a, r[1], b), core) for a, b in steps] for r in routes]
    line = [[device(moved(r[2], o), core) for o in (1, 2, 3)] for r in routes]

    def block_copy(n):
        rows = pl.ds(8 * n, 8)
        return pltpu.make_async_copy(block_inverse.at[rows], bvm.at[rows], b_sem.at[n])

    arriving = [
        pltpu.make_async_copy(src, dst, in_sem.at[n])
        for n, (src, dst) in enumerate(
            (
                (kappa_in, kappa), (rhs_in, rhs), (mass_ref_in, mass_ref), (stiff_ref_in, stiff_ref),
                (face_mass_in, face_mass), (modes_t_in, modes_t), (elem_agg_in, elem_agg), (mass_coef_in, mass_coef),
                (coarse_diag_in, coarse_diag), (coarse_inv_in, coarse_inv),
                (coarse_weight_in, coarse_weight), (coarse_links_in, coarse_links),
            )
        )
    ]
    for copy in arriving:
        copy.start()
    for n in range(8):
        block_copy(n).start()

    barrier = pltpu.get_barrier_semaphore()
    greeted = list(beside) + [sibling] + plane[0] + plane[1]
    for target in greeted:
        pl.semaphore_signal(barrier, inc=1, device_id=target, device_id_type=MESH)
    pl.semaphore_wait(barrier, len(greeted))

    def remote(src, dst, send, recv, target):
        return pltpu.make_async_remote_copy(
            src_ref=src, dst_ref=dst, send_sem=send, recv_sem=recv, device_id=target, device_id_type=MESH
        )

    exists = (gx > 0, gx < 3, gy > 0, gy < 3, gz > 0, gz < 7)

    def kappa_copy(f):
        return remote(kappa, krecv.at[f ^ 1], k_send.at[f], k_recv.at[f ^ 1], beside[f])

    arriving[0].wait()
    for f in range(6):
        pl.when(exists[f])(lambda: kappa_copy(f).start())

        @pl.when(jnp.logical_not(exists[f]))
        def _():
            krecv[f] = jnp.zeros((16, 128), F32)
            for slot in range(2):
                if f < 4:
                    rx[slot, f] = jnp.zeros((64, 128), F32)
                else:
                    rz[slot, f - 4] = jnp.zeros((16, 128), F32)

    arriving[1].wait()
    wm[...] = jnp.zeros_like(wm)
    for d in range(64):
        part = rhs[pl.ds(d * 16, 16), :]
        td[of_dof(d % 4, d // 4), :] = part
        rb[d] = part.astype(BF16)

    half = iota((8, 128), 0) < 4
    lane16 = iota((16, 128), 1)

    def face_copy(f, slot):
        if f < 4:
            src, dst = sx.at[f], rx.at[slot, f ^ 1]
        else:
            src, dst = sz.at[f - 4], rz.at[slot, (f ^ 1) - 4]
        return remote(src, dst, h_send.at[f], h_recv.at[slot, f ^ 1], beside[f])

    def send(f, slot):
        pl.when(exists[f])(lambda: face_copy(f, slot).start())

    def send_x(slot):
        for y in range(4):
            for pair in range(2):
                at = pl.ds(y * 16 + pair * 8, 8)
                low, up = y * 64 + 32 * pair, (12 + y) * 64 + 32 * pair + 8
                sx[XL, at, :] = jnp.where(half, wm[pl.ds(low, 8), :], pltpu.roll(wm[pl.ds(low + 16, 8), :], 4, 0))
                sx[XU, at, :] = jnp.where(half, pltpu.roll(wm[pl.ds(up, 8), :], 4, 0), wm[pl.ds(up + 16, 8), :])
        send(XL, slot)
        send(XU, slot)

    def send_y(slot):
        for x in range(4):
            at = pl.ds(x * 16, 16)
            sx[YL, at, :] = wm[pl.ds(4 * x * 64, 16, stride=4), :]
            sx[YU, at, :] = wm[pl.ds((4 * x + 3) * 64 + 3, 16, stride=4), :]
        send(YL, slot)
        send(YU, slot)

    def send_z(slot):
        def packed(first, lane):
            place_in = (lane16 - lane) & 127
            parts = [wm[pl.ds(xy * 64 + first, 16), :] for xy in range(16)]
            for bit in (1, 2, 4, 8):
                odd = (place_in & bit) != 0
                parts = [jnp.where(odd, pltpu.roll(b, bit, 1), a) for a, b in zip(parts[::2], parts[1::2])]
            return pltpu.roll(parts[0], 128 - lane, 1) if lane else parts[0]

        sz[0] = packed(0, 0)
        sz[1] = packed(48, 127)
        send(ZL, slot)
        send(ZU, slot)

    def spot(xy):
        x, y = xy // 4, xy % 4
        return (2 * x, y - 1) if y in (1, 2) else (2 * x + 1, y // 3)

    def operate(slot):
        def put(xy, at, count, which, value):
            pair, h = spot(xy)
            lanes = pl.ds(h * 128, 128)
            value = coef[which, pl.ds(xy, 1), :] * value
            high = value.astype(BF16)
            zhi[pair, pl.ds(at, count), lanes] = high
            zlo[pair, pl.ds(at, count), lanes] = (value - high.astype(F32)).astype(BF16)

        for xy in range(16):
            x, y = xy // 4, xy % 4
            here = wm[pl.ds(xy * 64, 64), :]
            put(xy, ROW_MASS, 64, 0, here)
            put(xy, ROW_STIFF, 64, 1, here)
            if x > 0:
                low = [wm[pl.ds((xy - 4) * 64 + 16 * k + 8, 8), :] for k in range(4)]
                put(xy, ROW_XL, 32, 2, jnp.concatenate(low, axis=0))
            if x < 3:
                up = [wm[pl.ds((xy + 4) * 64 + 16 * k, 8), :] for k in range(4)]
                put(xy, ROW_XU, 32, 3, jnp.concatenate(up, axis=0))
            if y > 0:
                put(xy, ROW_YL, 16, 4, wm[pl.ds((xy - 1) * 64 + 3, 16, stride=4), :])
            if y < 3:
                put(xy, ROW_YU, 16, 5, wm[pl.ds((xy + 1) * 64, 16, stride=4), :])

        def arrived(*places):
            for f in places:

                @pl.when(exists[f])
                def _():
                    face_copy(f, slot).wait_send()
                    face_copy(f ^ 1, slot).wait_recv()

        def store(xy, left, last):
            dm[pl.ds(xy * 64, 64), :] = left
            if last:
                td[of_element(xy), :] = left

        def apply(pair):
            both = bf16_dot(whl[...], zhi[pair])
            applied = both[0:64] + (both[64:128] + bf16_dot(whl[pl.ds(0, 64), :], zlo[pair]))
            for xy in range(16):
                if spot(xy)[0] == pair:
                    h = spot(xy)[1]
                    store(xy, rhsm[pl.ds(xy * 64, 64), :] - applied[:, h * 128 : h * 128 + 128], False)

        def from_beside(f, elements, last):
            parts = [
                split(coef[2 + f, pl.ds(xy, 1), :] * rx[slot, f, pl.ds((xy % 4 if f < 2 else xy // 4) * 16, 16), :])
                for xy in elements
            ]
            high, low = (jnp.concatenate([parts[0][n], parts[1][n]], axis=1) for n in range(2))
            added = bf16_dot(wf[f], jnp.concatenate([high, low, high, high], axis=0))
            for h, xy in enumerate(elements):
                store(xy, dm[pl.ds(xy * 64, 64), :] - added[:, h * 128 : h * 128 + 128], last)

        for xy in range(16):
            below = pltpu.roll(wm[pl.ds(xy * 64 + 48, 16), :], 1, 1)
            above = pltpu.roll(wm[pl.ds(xy * 64, 16), :], 127, 1)
            put(xy, ROW_ZL, 16, 6, jnp.where(lane16 == 0, 0.0, below))
            put(xy, ROW_ZU, 16, 7, jnp.where(lane16 == 127, 0.0, above))
        for pair in range(8):
            apply(pair)
        arrived(ZL, ZU)
        for n, first, lane in ((0, 0, 0), (1, 48, 127)):
            high, low = split(coef_z[pl.ds(n, 1), :] * rz[slot, n])
            added = bf16_dot(wz[...], jnp.concatenate([high, low, high, high], axis=0))
            for xy in range(16):
                rows = pl.ds(xy * 64 + first, 16)
                at_lane = jnp.where(lane16 == lane, pltpu.roll(added, (lane - xy) % 128, 1), 0.0)
                dm[rows, :] = dm[rows, :] - at_lane
        for xy in (5, 6, 9, 10):
            td[of_element(xy), :] = dm[pl.ds(xy * 64, 64), :]
        arrived(XL, XU)
        for f, at in ((XL, 0), (XU, 12)):
            from_beside(f, (at + 1, at + 2), True)
            from_beside(f, (at, at + 3), False)
        arrived(YL, YU)
        for f, at in ((YL, 0), (YU, 3)):
            from_beside(f, (at, at + 4), True)
            from_beside(f, (at + 8, at + 12), True)

    adder = (iota((16, 256), 1) % 16 == iota((16, 256), 0)).astype(F32).astype(BF16)

    def block_rows(dofs):
        groups = [[], [], [], []]
        for g in range(16):
            column = [rb[4 * g + j] for j in range(4)]
            for i, (k, q) in enumerate(dofs):
                m = [bvm[4 * q + k, 4 * g + j] * column[j] for j in range(4)]
                groups[i].append((m[0] + m[1]) + (m[2] + m[3]))
        rows = [jnp.concatenate(g, axis=0) for g in groups]
        for pair in range(2):
            sums = bf16_dot(adder, jnp.concatenate(rows[2 * pair : 2 * pair + 2], axis=1))
            for i in range(2):
                k, q = dofs[2 * pair + i]
                tw[of_dof(k, q), :] = damping * sums[:, 128 * i : 128 * i + 128]

    def outer(n):
        block_rows([(0, 2 * n), (3, 2 * n), (0, 2 * n + 1), (3, 2 * n + 1)])

    def middle(q, r):
        block_rows([(1, q), (2, q), (1, r), (2, r)])

    def add_update(first, count):
        for xy in range(16):
            rows = pl.ds(xy * 64 + first, count)
            wm[rows, :] = wm[rows, :] + tw[of_element(xy, first, count), :]

    def sweep(slot):
        pl.loop(0, 8)(outer)
        add_update(0, 16)
        add_update(48, 16)
        send_z(slot)
        pl.loop(0, 4)(lambda n: middle(2 * n + 8 * (n // 2), 2 * n + 8 * (n // 2) + 1))
        pl.loop(0, 2)(lambda n: middle(4 + 4 * n, 7 + 4 * n))
        for k in (1, 2):
            for q in (5, 6, 9, 10):
                tw[of_dof(k, q), :] = jnp.zeros((16, 128), F32)
        add_update(16, 32)
        send_x(slot)
        send_y(slot)
        pl.loop(0, 2)(lambda n: middle(5 + 4 * n, 6 + 4 * n))
        sub = iota((8, 128), 0)
        off_face = ((sub == 5) | (sub == 6), (sub == 1) | (sub == 2))
        for xy in range(16):
            for v in range(4):
                rows = pl.ds(xy * 64 + 16 + 8 * v, 8)
                wm[rows, :] = wm[rows, :] + jnp.where(off_face[v % 2], tw[of_element(xy, 16 + 8 * v, 8), :], 0.0)

    def first_sweep(slot):
        @pl.loop(0, 8)
        def _(n):
            block_copy(n).wait()
            outer(n)
            middle(2 * n, 2 * n + 1)

        add_update(0, 64)
        send_z(slot)
        send_x(slot)
        send_y(slot)

    first_sweep(0)

    for copy in arriving[2:]:
        copy.wait()

    for xy in range(16):
        rhsm[pl.ds(xy * 64, 64), :] = td[of_element(xy), :]
    high, low = split(stacked_operator(mass_ref[...], stiff_ref[...], face_mass[...]))
    whl[pl.ds(0, 64), :] = high
    whl[pl.ds(64, 64), :] = low
    col = iota((256, 256), 1)
    face, part, c = col // 64, col % 64 // 16, col % 16
    along_x = jnp.where(face == 0, ROW_XL + 4, ROW_XU) + c // 4 * 8 + c % 4
    along_y = jnp.where(face == 2, ROW_YL, ROW_YU) + c
    chosen = iota((256, 256), 0) == jnp.where(face < 2, along_x, along_y)
    taken = bf16_dot(high, (chosen & (part < 2)).astype(F32).astype(BF16))
    taken = taken + bf16_dot(low, (chosen & (part == 2)).astype(F32).astype(BF16))
    for f in range(4):
        wf[f] = taken[:, 64 * f : 64 * f + 64].astype(BF16)
    col = iota((256, 64), 1)
    part, chosen = col // 16, iota((256, 64), 0) == ROW_ZL + col % 16
    taken = bf16_dot(high[0:16], (chosen & (part < 2)).astype(F32).astype(BF16))
    taken = taken + bf16_dot(low[0:16], (chosen & (part == 2)).astype(F32).astype(BF16))
    wz[...] = taken.astype(BF16)
    zhi[...] = jnp.zeros_like(zhi)
    zlo[...] = jnp.zeros_like(zlo)
    ordered = (iota((64, 64), 0) == row_of(iota((64, 64), 1))).astype(F32)
    modes = exact_dot(ordered, modes_t[...], (((1,), (1,)), ((), ())))
    mt_hi, mt_lo = split(exact_dot(modes_t[...], ordered, (((1,), (1,)), ((), ()))))
    for f in range(6):

        @pl.when(exists[f])
        def _():
            kappa_copy(f).wait_send()
            kappa_copy(f ^ 1).wait_recv()

    own = kappa[...]
    row, lane = iota((16, 128), 0), iota((16, 128), 1)
    down_x = jnp.concatenate([krecv[XL][12:16], own[0:12]], axis=0)
    up_x = jnp.concatenate([own[4:16], krecv[XU][0:4]], axis=0)
    down_y = jnp.where(row % 4 == 0, jnp.roll(krecv[YL], -3, 0), jnp.roll(own, 1, 0))
    up_y = jnp.where(row % 4 == 3, jnp.roll(krecv[YU], 3, 0), jnp.roll(own, -1, 0))
    down_z = jnp.where(lane == 0, pltpu.roll(krecv[ZL], 1, 1), pltpu.roll(own, 1, 1))
    up_z = jnp.where(lane == 127, pltpu.roll(krecv[ZU], 127, 1), pltpu.roll(own, 127, 1))
    outside = (
        (row < 4) & (gx == 0), (row >= 12) & (gx == 3),
        (row % 4 == 0) & (gy == 0), (row % 4 == 3) & (gy == 3),
        (lane == 0) & (gz == 0), (lane == 127) & (gz == 7),
    )
    coef[0] = mass_coef[...]
    coef[1] = own
    for f, near in enumerate((down_x, up_x, down_y, up_y, down_z, up_z)):
        near = jnp.where(outside[f], 0.0, near)
        coef[2 + f] = 2.0 * own * near / (own + near)
    here = (row == lane).astype(F32)
    coef_z[0:1, :] = jnp.sum(here * coef[6][:, 0:1], axis=0, keepdims=True)
    coef_z[1:2, :] = jnp.sum(here * coef[7][:, 127:128], axis=0, keepdims=True)

    def coarse_setup():
        turned = (iota((64, 64), 1) == iota((64, 64), 0) % 8 * 8 + iota((64, 64), 0) // 8).astype(F32)
        inv_t[...] = exact_dot(turned, coarse_inv[...])
        diag_t[...] = exact_dot(turned, coarse_diag[...])
        agg = elem_agg[...]
        eye128 = (iota((128, 128), 0) == iota((128, 128), 1)).astype(F32)
        agg_t = exact_dot(eye128, agg.astype(F32), (((1,), (1,)), ((), ())))
        numbers = iota((128, 256), 1).astype(F32)
        for xy in range(16):
            mem[pl.ds(xy * 128, 128), :] = (agg_t[:, xy : xy + 1] == numbers).astype(F32).astype(BF16)

    def whole(cycle, half_id, which, done, chip):
        index = [slice(None) if d in done else chip[d] for d in range(3)]
        return held.at[cycle, which, index[2], index[1], index[0], half_id]

    def plane_copy(cycle, half_id, n):
        block = whole(cycle, half_id, core, (), place)
        at = (cycle, half_id, n)
        return remote(block, block, p_send.at[at], p_recv.at[at], plane[half_id][n])

    def line_copy(cycle, half_id, o):
        block = whole(cycle, half_id, core, routes[half_id][:2], place)
        at = (cycle, half_id, o - 1)
        return remote(block, block, g_send.at[at], g_recv.at[at], line[half_id][o - 1])

    def sibling_copy(cycle, half_id, o):
        route = routes[half_id]
        chip = moved(route[2], -o)
        block = whole(cycle, half_id, core, route[:2], chip)
        at = (cycle, half_id, o)
        return remote(block, block, d_send.at[at], d_recv.at[at], sibling)

    def collect(cycle, state):
        for h in range(2):
            held[cycle, core, place[2], place[1], place[0], h] = state[:, h * 128 : h * 128 + 128]

        for n in range(15):
            for h in range(2):
                plane_copy(cycle, h, n).start()
        @pl.when(cycle == 0)
        def _():
            links = coarse_links[...]
            for f in range(4):
                picked[f] = ((links[f : f + 1, :] & 127) == (iota((256, 256), 0) & 127)).astype(F32).astype(BF16)
            for f in range(6):
                chunk_of[f] = jnp.broadcast_to(links[f : f + 1, :] >> 7, (8, 256))
            numbers_t = iota((256, 128), 0)
            for xy in range(16):
                mem_t[:, pl.ds(xy * 128, 128)] = (elem_agg[pl.ds(xy, 1), :] == numbers_t).astype(F32).astype(BF16)

        for h in range(2):
            for n in range(15):
                plane_copy(cycle, h, n).wait_recv()
            for o in (1, 2, 3):
                line_copy(cycle, h, o).start()
        for h in range(2):
            sibling_copy(cycle, h, 0).start()

        lanes = [
            jnp.broadcast_to(coarse_links[f : f + 1, h * 128 : h * 128 + 128] & 127, (8, 128)) for f in (4, 5) for h in range(2)
        ]
        chunks = [chunk_of[f, :, h * 128 : h * 128 + 128] for f in range(6) for h in range(2)]

        def look(found, which, o):
            numbers, values = [], []
            for half_id in range(2):
                route = routes[half_id]
                chip = moved(route[2], -o)
                for n in range(16):
                    x, y, z = (n // 4 if d == route[0] else n % 4 if d == route[1] else chip[d] for d in range(3))
                    numbers.append((((z % 2) * 2 + which) * 32 + y * 8 + x * 2 + z // 2) * 2 + half_id)
                    values.append(held[cycle, which, z, y, x, half_id])
            lhs = jnp.concatenate(split(jnp.concatenate(values, axis=0)), axis=1)
            found = list(found)

            def choose(into, value_of):
                parts = []
                for first in range(0, 32, 8):
                    part = jnp.zeros((8, 128), F32)
                    for n in range(first, first + 8):
                        part = jnp.where(chunks[into] == numbers[n], value_of(n), part)
                    parts.append(part)
                found[into] = found[into] + ((parts[0] + parts[1]) + (parts[2] + parts[3]))

            for f in range(4):
                at_lane = bf16_dot(lhs, picked[f])
                choose(8 + f, lambda n: jnp.take_along_axis(values[n], lanes[f], axis=1))
                for h in range(2):
                    choose(2 * f + h, lambda n: at_lane[8 * n : 8 * n + 8, 128 * h : 128 * h + 128])
            return found

        found = look([jnp.zeros((8, 128), F32) for _ in range(12)], core, 0)
        for h in range(2):
            sibling_copy(cycle, h, 0).wait_recv()
        found = look(found, 1 - core, 0)
        for o in (1, 3, 2):
            for h in range(2):
                line_copy(cycle, h, o).wait_recv()
                sibling_copy(cycle, h, o).start()
        for o in (1, 3, 2):
            found = look(found, core, o)
        for o in (1, 3, 2):
            for h in range(2):
                sibling_copy(cycle, h, o).wait_recv()
        for o in (1, 3, 2):
            found = look(found, 1 - core, o)
        weight = coarse_weight[...]
        total = jnp.zeros((8, 256), F32)
        for f in range(6):
            total = total + weight[f : f + 1, :] * jnp.concatenate(found[2 * f : 2 * f + 2], axis=1)
        return total

    def collect_end(cycle):
        for h in range(2):
            for n in range(15):
                plane_copy(cycle, h, n).wait_send()
            for o in (1, 2, 3):
                line_copy(cycle, h, o).wait_send()
            for o in range(4):
                sibling_copy(cycle, h, o).wait_send()

    def coarse_product(blocks, state):
        total = blocks[pl.ds(0, 8), :] * state[0:1, :]
        for j in range(1, 8):
            total = total + blocks[pl.ds(8 * j, 8), :] * state[j : j + 1, :]
        return total

    def coarse(cycle, slot):
        left = jnp.concatenate([mt_hi, mt_hi, mt_lo], axis=1)
        for pair in range(8):
            both = [split(dm[pl.ds((2 * pair + h) * 64, 64), :]) for h in range(2)]
            highs = jnp.concatenate([both[0][0], both[1][0]], axis=1)
            lows = jnp.concatenate([both[0][1], both[1][1]], axis=1)
            projected = bf16_dot(left, jnp.concatenate([highs, lows, highs], axis=0))
            p_hi, p_lo = split(projected)
            pj[:, pl.ds(pair * 256, 256)] = jnp.concatenate([p_hi, p_lo], axis=0)
        summed = bf16_dot(pj[...], mem[...])
        restricted = summed[0:8] + summed[8:16]
        state = damping * coarse_product(inv_t, restricted)
        applied = coarse_product(diag_t, state) - collect(cycle, state)
        state = state + damping * coarse_product(inv_t, restricted - applied)
        s_hi, s_lo = split(exact_dot(modes, state))
        stacked = jnp.concatenate([s_hi, s_lo], axis=0)
        for pair in range(8):
            both = bf16_dot(stacked, mem_t[:, pl.ds(pair * 256, 256)])
            spread = both[0:64] + both[64:128]
            for h in range(2):
                rows = pl.ds((2 * pair + h) * 64, 64)
                wm[rows, :] = wm[rows, :] + spread[:, h * 128 : h * 128 + 128]
        send_z(slot)
        send_x(slot)
        send_y(slot)
        collect_end(cycle)

    @pl.loop(0, 9)
    def _(t):
        slot = t % 2
        operate(slot)

        @pl.when(t % 5 == 1)
        def _():
            coarse(t // 5, 1 - slot)

        @pl.when(t % 5 != 1)
        def _():
            for d in range(64):
                rb[d] = td[of_dof(d % 4, d // 4), :].astype(BF16)
            sweep(1 - slot)
            pl.when(t == 0)(coarse_setup)

    def leave(n, source, target):
        for d in range(64):
            leaving[n, pl.ds(d * 16, 16), :] = source[of_dof(d % 4, d // 4), :]
        return pltpu.make_async_copy(leaving.at[n], target, out_sem.at[n])

    for xy in range(16):
        tw[of_element(xy), :] = wm[pl.ds(xy * 64, 64), :]
    first_out = leave(0, tw, sol_out)
    first_out.start()
    operate(1)
    second_out = leave(1, td, res_out)
    second_out.start()
    first_out.wait()
    second_out.wait()


def write_out(first, second, first_out, second_out, held, in_sems, out_sems):
    parts = [(m, pl.ds(n * 256, 256), n) for m in range(2) for n in range(4)]
    ends = ((first, first_out), (second, second_out))
    into = [pltpu.make_async_copy(ends[m][0].at[at], held.at[m, at], in_sems.at[m, n]) for m, at, n in parts]
    out = [pltpu.make_async_copy(held.at[m, at], ends[m][1].at[at], out_sems.at[m, n]) for m, at, n in parts]
    for copy in into:
        copy.start()
    for arriving, leaving in zip(into, out):
        arriving.wait()
        leaving.start()
    for copy in out:
        copy.wait()


def on_device(
    right_side, mass_coef, conductivity, block_inverse, mass_ref, stiff_ref, face_mass, coarse_modes, elem_agg,
    coarse_diag, coarse_inv, coarse_weight, coarse_links,
):
    far = pl.BlockSpec(memory_space=pltpu.HBM)
    dma = pltpu.SemaphoreType.DMA
    shape = right_side.shape
    flat = jax.ShapeDtypeStruct((1024, 128), F32)
    solution_now, residual = pl.pallas_call(
        kernel,
        out_shape=(flat, flat),
        in_specs=[far] * 13,
        out_specs=(far, far),
        scratch_shapes=[
            pltpu.VMEM((1024, 128), F32),
            pltpu.VMEM((16, 128), F32),
            pltpu.VMEM((16, 128), F32),
            pltpu.VMEM((64, 64), F32),
            pltpu.VMEM((64, 64), F32),
            pltpu.VMEM((16, 16), F32),
            pltpu.VMEM((8, 64), F32),
            pltpu.VMEM((16, 128), jnp.int32),
            pltpu.VMEM((64, 256), F32),
            pltpu.VMEM((64, 256), F32),
            pltpu.VMEM((6, 256), F32),
            pltpu.VMEM((6, 256), jnp.int32),
            pltpu.VMEM((64, 64, 16, 128), BF16),
            pltpu.VMEM((1024, 128), F32),
            pltpu.VMEM((1024, 128), F32),
            pltpu.VMEM((64 * DOF_STEP, 128), F32),
            pltpu.VMEM((64 * DOF_STEP, 128), F32),
            pltpu.VMEM((1024, 128), F32),
            pltpu.VMEM((64, 16, 128), BF16),
            pltpu.VMEM((64, 256), F32),
            pltpu.VMEM((64, 256), F32),
            pltpu.VMEM((8, 256, 256), BF16),
            pltpu.VMEM((8, 256, 256), BF16),
            pltpu.VMEM((128, 256), BF16),
            pltpu.VMEM((4, 64, 64), BF16),
            pltpu.VMEM((16, 64), BF16),
            pltpu.VMEM((2, 128), F32),
            pltpu.VMEM((8, 16, 128), F32),
            pltpu.VMEM((2048, 256), BF16),
            pltpu.VMEM((256, 2048), BF16),
            pltpu.VMEM((4, 256, 256), BF16),
            pltpu.VMEM((6, 8, 256), jnp.int32),
            pltpu.VMEM((16, 2048), BF16),
            pltpu.VMEM((2, 4, 64, 128), F32),
            pltpu.VMEM((2, 2, 16, 128), F32),
            pltpu.VMEM((4, 64, 128), F32),
            pltpu.VMEM((2, 16, 128), F32),
            pltpu.VMEM((6, 16, 128), F32),
            pltpu.VMEM((2, 2, 4, 4, 4, 2, 8, 128), F32),
            pltpu.VMEM((2, 1024, 128), F32),
            dma((2,)),
            dma((12,)),
            dma((8,)),
            dma((6,)),
            dma((6,)),
            dma((6,)),
            dma((2, 6)),
            dma((2, 2, 15)),
            dma((2, 2, 15)),
            dma((2, 2, 3)),
            dma((2, 2, 3)),
            dma((2, 2, 4)),
            dma((2, 2, 4)),
        ],
        compiler_params=pltpu.CompilerParams(
            collective_id=0, has_side_effects=True, vmem_limit_bytes=63 * 1024 * 1024
        ),
    )(
        right_side.reshape(1024, 128),
        mass_coef.reshape(16, 128),
        conductivity.reshape(16, 128),
        block_inverse.reshape(64, 64, 16, 128),
        mass_ref,
        stiff_ref,
        face_mass,
        coarse_modes.T,
        elem_agg.reshape(16, 128),
        coarse_diag.reshape(64, 256),
        coarse_inv.reshape(64, 256),
        coarse_weight,
        coarse_links,
    )
    solution_now, residual = pl.pallas_call(
        write_out,
        out_shape=(flat, flat),
        in_specs=[far] * 2,
        out_specs=(far, far),
        scratch_shapes=[pltpu.VMEM((2, 1024, 128), F32), dma((2, 4)), dma((2, 4))],
        compiler_params=pltpu.CompilerParams(vmem_limit_bytes=63 * 1024 * 1024),
    )(solution_now, residual)
    return solution_now.reshape(shape), residual.reshape(shape)


def solution(mesh):
    split_all = ("gx", "gy", "gz")
    return jax.shard_map(
        on_device,
        mesh=mesh,
        in_specs=(
            P(None, None, None, "gx", "gy", "gz"),
            P("gx", "gy", "gz"),
            P("gx", "gy", "gz"),
            P(None, None, "gx", "gy", "gz"),
            P(),
            P(),
            P(),
            P(),
            P("gx", "gy", "gz"),
            P(None, None, split_all),
            P(None, None, split_all),
            P(None, split_all),
            P(None, split_all),
        ),
        out_specs=(P(None, None, None, "gx", "gy", "gz"), P(None, None, None, "gx", "gy", "gz")),
        check_vma=False,
    )
```
